128 devices in a mesh: blk: 8 (over x, z_lo), cuts: 16 (over y, z_hi, core).
Axes of the slice: x: 4, y: 4, z: 4 (z_hi: 2, z_lo: 2; z = z_hi * 2 + z_lo), core: 2. Of those that a mesh axis runs over, the one named last changes fastest.
Arguments:
- summaries: bfloat16 [16384, 5120], P('blk', 'cuts')
- head: bfloat16 [5120, 1024], P('cuts'), may hold values from -0.078125 to 0.078125
- partner: int32 [16384], P('blk'), may hold values from 0 to 16383, as said below
Outputs:
- loss: float32 [], replicated
- grad_summaries: bfloat16 [16384, 5120], P('blk', 'cuts')
- grad_head: float32 [5120, 1024], P('cuts')
The draws below stay inside these ranges and needn't reach their ends.
Inputs may be any that keep to these rules, and one draw needn't show every extreme that they name: partner pairs the rows: partner[partner[i]] = i and partner[i] != i for every row i.
All inputs are finite; a program needn't handle non-finite values.
Results may differ from the reference program's by a relative error of at most 0.017.
Values may be sent and summed in bfloat16 or wider, within the bound.
No kernel may reach another device: no remote copies, remote signals or barrier semaphores. Data moves between devices by JAX's collectives and lax.ppermute only.
A program may use at most 64 MiB of HBM per device.

```python
import math
import jax
import jax.numpy as jnp
from jax import lax

D = 5120
P_SIZE = 1024
N = 16384
GROUP = 2048
N_BLK = 8


def pair_order(key):
    return jax.random.permutation(jax.random.fold_in(key, 5), N).astype(jnp.int32)


def draw_summaries(key, part):
    order = pair_order(key)
    key = jax.random.fold_in(key, 11)
    centre_key, offset_key, noise_key, scale_key = jax.random.split(key, 4)
    rank = jnp.zeros((N,), jnp.int32).at[order].set(jnp.arange(N, dtype=jnp.int32))
    cluster = rank // 8
    couple = rank // 2
    centres = jnp.clip(jax.random.normal(centre_key, (N // 8, D), jnp.float32), -6.0, 6.0)
    offsets = jnp.clip(jax.random.normal(offset_key, (N // 2, D), jnp.float32), -6.0, 6.0)
    noise = jnp.clip(jax.random.normal(noise_key, (N, D), jnp.float32), -6.0, 6.0)
    scale = jnp.exp(jax.random.uniform(scale_key, (N, 1), jnp.float32, math.log(0.01), math.log(0.1)))
    base = 0.71 * centres[cluster] + 0.45 * offsets[couple] + 0.55 * noise
    return (base * scale).astype(jnp.bfloat16)


def draw_partner(key, part):
    order = pair_order(key)
    first = order[0::2]
    second = order[1::2]
    mates = jnp.zeros((N,), jnp.int32)
    mates = mates.at[first].set(second)
    mates = mates.at[second].set(first)
    return mates


def level_of(rng, shape, shards, smallest, high):
    gain, own = 1.0, jax.random.fold_in(rng, 6)
    for axis_at, blocks in shards:
        draws = jnp.exp(jax.random.uniform(jax.random.fold_in(own, axis_at), (blocks,), jnp.float32, smallest / len(shards), high / len(shards)))
        gain = gain * jnp.repeat(draws, shape[axis_at] // blocks).reshape([-1 if axis == axis_at else 1 for axis in range(len(shape))])
    return gain


def normal_values(key, extent, spread, limit, shards=(), kind=jnp.bfloat16):
    level = level_of(key, extent, shards, -0.22, 0.18) if shards else 1.0
    drawn = jax.random.normal(key, extent, jnp.float32) * spread * level
    return jnp.minimum(jnp.maximum(drawn, -limit), limit).astype(kind)


def setup_inputs(seed: int = 0) -> dict:
    seeds = jax.random.split(jax.random.key(seed), 4)
    return {
        "summaries": draw_summaries(jax.random.fold_in(seeds[3], 71), 0),
        "head": normal_values(seeds[1], (D, P_SIZE), D ** -0.5, 0.078125, ((0, 16),)),
        "partner": draw_partner(jax.random.fold_in(seeds[3], 71), 0),
    }


def reference(summaries, head, partner):
    z = jnp.dot(summaries, head, preferred_element_type=jnp.float32)
    inv = lax.rsqrt(lax.optimization_barrier(jnp.sum(z * z, axis=1, keepdims=True)) + 1e-06)
    unit = z * inv
    emb = unit.astype(jnp.bfloat16)
    kglob = jnp.arange(N, dtype=jnp.int32)

    def block(key_acc, index):
        start = (index * GROUP).astype(jnp.int32)
        queries = lax.dynamic_slice_in_dim(emb, start, GROUP, 0)
        mates = lax.dynamic_slice_in_dim(partner, start, GROUP, 0)
        qglob = start + jnp.arange(GROUP, dtype=jnp.int32)
        scores = 20.0 * jnp.dot(queries, emb.T, preferred_element_type=jnp.float32)
        live = qglob[:, None] != kglob[None, :]
        weights = jnp.where(live, jnp.exp(scores), jnp.float32(0.0))
        hit = (mates[:, None] == kglob[None, :]).astype(jnp.float32)
        den = lax.optimization_barrier(jnp.sum(weights, axis=1))
        pos = lax.optimization_barrier(jnp.sum(scores * hit, axis=1))
        losses = jnp.log(den) - pos
        grad_scores = (20.0 * (weights / den[:, None] - hit)).astype(jnp.bfloat16)
        query_part = jnp.dot(grad_scores, emb, preferred_element_type=jnp.float32)
        key_acc = key_acc + jnp.dot(grad_scores.T, queries, preferred_element_type=jnp.float32)
        return (key_acc, (query_part, losses))
    key_acc, (query_part, losses) = lax.scan(block, jnp.zeros((N, P_SIZE), jnp.float32), jnp.arange(N_BLK, dtype=jnp.int32))
    grad_emb = query_part.reshape(N, P_SIZE) + key_acc
    grad_z = (inv * (grad_emb - unit * lax.optimization_barrier(jnp.sum(unit * grad_emb, axis=1, keepdims=True)))).astype(jnp.bfloat16)
    grad_summaries = jnp.dot(grad_z, head.T, preferred_element_type=jnp.float32).astype(jnp.bfloat16)
    grad_head = jnp.dot(summaries.T, grad_z, preferred_element_type=jnp.float32)
    loss = jnp.sum(losses) / N
    return (loss, grad_summaries, grad_head)
```

```python
import jax
import jax.numpy as jnp
from jax import lax
from jax.sharding import Mesh
from jax.sharding import PartitionSpec as P

F32 = jnp.float32
BF16 = jnp.bfloat16
SWAP = [(0, 1), (1, 0)]
RING = {s: [(i, (i + s) % 4) for i in range(4)] for s in (1, 2, 3)}


def core_swap(value):
    return lax.ppermute(value, "c", SWAP)


def gather_ring(own, long_axis, short_axis):
    rows = own.shape[0]
    other = lax.ppermute(own, short_axis, SWAP)
    first = lax.axis_index(short_axis) == 0
    pair = jnp.concatenate([jnp.where(first, own, other), jnp.where(first, other, own)], 0)
    after = lax.ppermute(pair, long_axis, RING[3])
    before = lax.ppermute(pair, long_axis, RING[1])
    far_top = lax.ppermute(after[:rows], long_axis, RING[3])
    far_low = lax.ppermute(before[rows:], long_axis, RING[1])
    at = lax.axis_index(long_axis)
    out = jnp.zeros((8 * rows, own.shape[1]), own.dtype)
    for shift, part, skip in (
        (0, pair, 0),
        (1, after, 0),
        (3, before, 0),
        (2, far_top, 0),
        (2, far_low, rows),
    ):
        start = lax.rem(at + shift, 4) * (2 * rows) + skip
        out = lax.dynamic_update_slice_in_dim(out, part, start, 0)
    return out


def sum_exchange(parts, axes):
    got = lax.all_to_all(parts, axes, 0, 0)
    return jnp.sum(got.astype(F32), axis=0)


def sum_everywhere(vector, axes):
    vector = vector.reshape(-1, 128)
    got = lax.all_to_all(jnp.broadcast_to(vector[None], (8,) + vector.shape), axes, 0, 0)
    return jnp.sum(got, axis=0).reshape(-1)


def shards(summaries, head, partner):
    yz, xz = ("y", "zh"), ("x", "zl")
    core = lax.axis_index("c")
    group_at = lax.axis_index("x") * 2 + lax.axis_index("zl")
    chunk_at = lax.axis_index("y") * 2 + lax.axis_index("zh")
    half = summaries.shape[0] // 2
    rows = half // 8
    width = head.shape[1]

    mine = lax.dynamic_slice_in_dim(summaries, core * half, half, 0)
    theirs = core_swap(lax.dynamic_slice_in_dim(summaries, (1 - core) * half, half, 0))
    other_head = core_swap(head)
    z_part = jnp.dot(mine, head, preferred_element_type=F32) + jnp.dot(
        theirs, other_head, preferred_element_type=F32
    )
    z = sum_exchange(z_part.astype(BF16).reshape(8, rows, width), yz)
    inv = lax.rsqrt(jnp.sum(z * z, axis=1, keepdims=True) + 1e-06)
    unit = z * inv
    emb = unit.astype(BF16)

    queries = gather_ring(emb, "y", "zh")
    keys_mine = gather_ring(emb, "x", "zl")
    keys = jnp.concatenate([keys_mine, core_swap(keys_mine)], 0)

    qglob = group_at * (2 * half) + core * half + jnp.arange(half, dtype=jnp.int32)
    local = jnp.arange(2 * half, dtype=jnp.int32)
    key_core = jnp.where(local < half, core, 1 - core)
    kglob = (local % half) // rows * (2 * half) + key_core * half + chunk_at * rows + local % rows
    mates = lax.dynamic_slice_in_dim(partner, core * half, half, 0)

    scores = 20.0 * lax.dot_general(
        queries, keys, (((1,), (1,)), ((), ())), preferred_element_type=F32
    )
    weights = jnp.where(qglob[:, None] != kglob[None, :], jnp.exp(scores), F32(0.0))
    hit = mates[:, None] == kglob[None, :]
    pos_part = jnp.sum(jnp.where(hit, scores, 0.0))
    row_part = jnp.sum(weights, axis=1)
    column_part = jnp.sum(weights, axis=0)
    swapped = core_swap(column_part.reshape(-1, 128)).reshape(-1)
    column_part = column_part + jnp.concatenate([swapped[half:], swapped[:half]])
    pos_row = jnp.zeros((1024,), F32).at[0].set(pos_part)
    row_sums = sum_everywhere(jnp.concatenate([row_part, pos_row]), yz)
    den_q, pos = row_sums[:half], row_sums[half]
    den_k = sum_everywhere(column_part, xz)

    grad_scores = (
        weights * ((20.0 / den_q)[:, None] + (20.0 / den_k)[None, :]) - jnp.where(hit, 40.0, 0.0)
    ).astype(BF16)
    grad_part = jnp.dot(grad_scores, keys, preferred_element_type=F32).astype(BF16)
    grad_emb = sum_exchange(grad_part.reshape(8, rows, width), yz)

    loss = jnp.full((8, 128), jnp.sum(jnp.log(den_q)) - pos, F32)
    loss = loss + core_swap(loss)
    loss = loss + lax.ppermute(loss, "zl", SWAP)
    loss = loss + lax.ppermute(loss, "x", RING[2])
    loss = loss + lax.ppermute(loss, "x", RING[1])
    loss = loss[0, 0] / (16 * half)

    grad_z = (inv * (grad_emb - unit * jnp.sum(unit * grad_emb, axis=1, keepdims=True))).astype(BF16)
    grad_half = gather_ring(grad_z, "y", "zh")

    contract_first = (((0,), (0,)), ((), ()))
    head_theirs = lax.dot_general(
        theirs, grad_half, contract_first, preferred_element_type=F32
    ).astype(BF16)
    head_mine = lax.dot_general(mine, grad_half, contract_first, preferred_element_type=F32)
    head_part = (head_mine + core_swap(head_theirs).astype(F32)).astype(BF16)
    features = head.shape[0]
    pieces = head_part.reshape(features, 8, width // 8).transpose(1, 0, 2)
    head_sum = sum_exchange(pieces, xz).astype(BF16)
    spread = lax.all_to_all(jnp.broadcast_to(head_sum[None], (8,) + head_sum.shape), xz, 0, 0)
    grad_head = spread.transpose(1, 0, 2).reshape(features, width).astype(F32)

    contract_last = (((1,), (1,)), ((), ()))
    out_theirs = lax.dot_general(
        other_head, grad_half, contract_last, preferred_element_type=F32
    ).astype(BF16)
    out_mine = lax.dot_general(head, grad_half, contract_last, preferred_element_type=F32).astype(BF16)
    got = core_swap(out_theirs)
    first = core == 0
    out = jnp.concatenate([jnp.where(first, out_mine, got), jnp.where(first, got, out_mine)], 1)
    return loss, out.T, grad_head


def solution(mesh):
    fine = Mesh(mesh.devices.reshape(4, 2, 4, 2, 2), ("x", "zl", "y", "zh", "c"))
    blk, cuts = ("x", "zl"), ("y", "zh", "c")
    return jax.shard_map(
        shards,
        mesh=fine,
        in_specs=(P(blk, cuts), P(cuts, None), P(blk)),
        out_specs=(P(), P(blk, cuts), P(cuts, None)),
        check_vma=False,
    )
```

```python
import jax
import jax.numpy as jnp
from jax import lax
from jax.experimental import pallas as pl
from jax.experimental.pallas import tpu as pltpu
from jax.sharding import Mesh
from jax.sharding import PartitionSpec as P

F32 = jnp.float32
BF16 = jnp.bfloat16
I32 = jnp.int32
SWAP = [(0, 1), (1, 0)]
ROWS = 128
HALF = 1024
GROUP = 2048
TOTAL = 16384
WIDTH = 1024
PART = 512
VMEM_LIMIT = 40 * 1024 * 1024
YZ, XZ, CUTS = ("y", "zh"), ("x", "zl"), ("y", "zh", "c")


def core_swap(value):
    return lax.ppermute(value, "c", SWAP)


def spread(value, axes, count):
    return lax.all_to_all(jnp.broadcast_to(value[None], (count,) + value.shape), axes, 0, 0)


def sum_exchange(parts, axes):
    return jnp.sum(lax.all_to_all(parts, axes, 0, 0).astype(F32), axis=0)


def key_ids(place, tile):
    zl = jnp.where(tile < 4, place[1], 1 - place[1])
    base = (lax.rem(tile, 4) * 2 + zl) * GROUP + place[4] * HALF + (place[2] * 2 + place[3]) * ROWS
    return base + lax.broadcasted_iota(I32, (ROWS, 1), 0)


def query_block(place, n):
    core = place[4] if n < 2 else 1 - place[4]
    zh = place[3] if n % 2 == 0 else 1 - place[3]
    return core, zh, core * 2 + zh


def query_ids(place, n):
    core, zh, _ = query_block(place, n)
    base = (place[0] * 2 + place[1]) * GROUP + core * HALF + zh * ROWS
    at = lax.broadcasted_iota(I32, (1, PART), 1)
    return base + (at // ROWS) * (2 * ROWS) + at % ROWS


def score_kernel(place, ka, kb, q0, q1, q2, q3, mates, w_ref, row_ref, col_ref):
    tile = pl.program_id(0)
    kid = key_ids(place, tile)

    @pl.when(tile == 0)
    def _():
        col_ref[...] = jnp.zeros_like(col_ref)

    def run(source, first):
        keys = source[pl.ds((tile - first) * ROWS, ROWS), :]
        row = jnp.zeros((ROWS, 1), F32)
        for n, q in enumerate((q0, q1, q2, q3)):
            block = query_block(place, n)[2]
            scores = 20.0 * lax.dot_general(
                keys, q[...], (((1,), (1,)), ((), ())), preferred_element_type=F32
            )
            weights = jnp.where(kid != query_ids(place, n), jnp.exp(scores), 0.0)
            w_ref[:, n * PART : (n + 1) * PART] = weights
            row = row + jnp.sum(weights, axis=1, keepdims=True)
            hits = jnp.where(kid == mates[block], scores, 0.0)
            col_ref[block, 0:8, :] += jnp.sum(weights.reshape(ROWS // 8, 8, PART), axis=0)
            col_ref[block, 8:16, :] += jnp.sum(hits.reshape(ROWS // 8, 8, PART), axis=0)
        row_ref[0] = row

    @pl.when(tile < 4)
    def _():
        run(ka, 0)

    @pl.when(tile >= 4)
    def _():
        run(kb, 4)


def grad_kernel(place, w_ref, rk_ref, rq_ref, mates, q0, q1, q2, q3, out_ref):
    tile = pl.program_id(0)
    kid = key_ids(place, tile)
    total = jnp.zeros((ROWS, WIDTH), F32)
    for n, q in enumerate((q0, q1, q2, q3)):
        block = query_block(place, n)[2]
        weights = w_ref[:, n * PART : (n + 1) * PART]
        grads = weights * (rk_ref[0] + rq_ref[block]) - jnp.where(kid == mates[block], 40.0, 0.0)
        total = total + jnp.dot(grads.astype(BF16), q[...], preferred_element_type=F32)
    out_ref[0] = total.astype(BF16)


def whole(shape):
    return pl.BlockSpec(shape, lambda t, place: (0,) * len(shape))


def piece(t, place):
    return lax.rem(t, 4) * 2 + jnp.where(t < 4, place[1], 1 - place[1])


def score_call(place, ka, kb, queries, mates):
    half = whole((PART, WIDTH))
    return pl.pallas_call(
        score_kernel,
        grid_spec=pltpu.PrefetchScalarGridSpec(
            num_scalar_prefetch=1,
            grid=(8,),
            in_specs=[half] * 6 + [whole((4, 1, PART))],
            out_specs=[
                pl.BlockSpec((ROWS, GROUP), lambda t, place: (t, 0)),
                pl.BlockSpec((1, ROWS, 1), lambda t, place: (piece(t, place), 0, 0)),
                whole((4, 16, PART)),
            ],
        ),
        out_shape=[
            jax.ShapeDtypeStruct((HALF, GROUP), F32),
            jax.ShapeDtypeStruct((8, ROWS, 1), F32),
            jax.ShapeDtypeStruct((4, 16, PART), F32),
        ],
        compiler_params=pltpu.CompilerParams(vmem_limit_bytes=VMEM_LIMIT),
        cost_estimate=pl.CostEstimate(
            flops=2 * HALF * GROUP * WIDTH, bytes_accessed=14 << 20, transcendentals=HALF * GROUP
        ),
        name="scores",
    )(place, ka, kb, *queries, mates)


def grad_call(place, weights, rk, rq, mates, queries):
    half = whole((PART, WIDTH))
    return pl.pallas_call(
        grad_kernel,
        grid_spec=pltpu.PrefetchScalarGridSpec(
            num_scalar_prefetch=1,
            grid=(8,),
            in_specs=[
                pl.BlockSpec((ROWS, GROUP), lambda t, place: (t, 0)),
                pl.BlockSpec((1, ROWS, 1), lambda t, place: (piece(t, place), 0, 0)),
                whole((4, 1, PART)),
                whole((4, 1, PART)),
            ]
            + [half] * 4,
            out_specs=pl.BlockSpec(
                (1, ROWS, WIDTH), lambda t, place: (piece(t, place), 0, 0)
            ),
        ),
        out_shape=jax.ShapeDtypeStruct((8, ROWS, WIDTH), BF16),
        compiler_params=pltpu.CompilerParams(vmem_limit_bytes=VMEM_LIMIT),
        cost_estimate=pl.CostEstimate(
            flops=2 * HALF * GROUP * WIDTH, bytes_accessed=14 << 20, transcendentals=0
        ),
        name="grads",
    )(place, weights, rk, rq, mates, *queries)


def shards(summaries, head, partner):
    core, zh = lax.axis_index("c"), lax.axis_index("zh")
    place = jnp.stack([lax.axis_index(a) for a in ("x", "zl", "y", "zh", "c")]).astype(I32)
    mates = partner.reshape(2, 4, 2, ROWS).transpose(0, 2, 1, 3).reshape(4, 1, PART)

    mine = lax.dynamic_slice_in_dim(summaries, core * HALF, HALF, 0)
    theirs = core_swap(lax.dynamic_slice_in_dim(summaries, (1 - core) * HALF, HALF, 0))
    other_head = core_swap(head)
    z_part = jnp.dot(mine, head, preferred_element_type=F32) + jnp.dot(
        theirs, other_head, preferred_element_type=F32
    )
    z = sum_exchange(z_part.astype(BF16).reshape(8, ROWS, WIDTH), YZ)
    inv = lax.rsqrt(jnp.sum(z * z, axis=1, keepdims=True) + 1e-06)
    unit = z * inv
    emb = unit.astype(BF16)

    q_other = lax.ppermute(emb, "zh", SWAP)
    k_other = lax.ppermute(emb, "zl", SWAP)
    q_near, k_near = spread(emb, "y", 4), spread(emb, "x", 4)
    q_far, k_far = spread(q_other, "y", 4), spread(k_other, "x", 4)
    queries = [a.reshape(PART, WIDTH) for a in (q_near, q_far)]
    queries += [core_swap(a) for a in queries]
    weights, row_part, col_part = score_call(
        place, k_near.reshape(PART, WIDTH), k_far.reshape(PART, WIDTH), queries, mates
    )

    pos_part = jnp.sum(col_part[:, 8:])
    col_part = jnp.sum(col_part[:, :8], axis=1).reshape(16, 128)
    col_part = jnp.concatenate([col_part, jnp.full((8, 128), pos_part, F32)], 0)
    row_part = row_part.reshape(8, ROWS)
    col_part, row_part = lax.optimization_barrier((col_part, row_part))
    cols = jnp.sum(spread(col_part, CUTS, 16), axis=0)
    rows = jnp.sum(spread(row_part, XZ, 8), axis=0)
    den_q, pos = cols[:16], cols[16, 0]
    rk = (20.0 / rows).reshape(8, ROWS, 1)
    rq = (20.0 / den_q).reshape(4, 1, PART)
    grad_part = grad_call(place, weights, rk, rq, mates, queries)

    loss = jnp.full((8, 128), jnp.sum(jnp.log(den_q)) - pos, F32)
    loss = jnp.sum(spread(loss, XZ, 8), axis=0)[0, 0] / TOTAL

    grad_emb = sum_exchange(grad_part, XZ)
    grad_emb, loss = lax.optimization_barrier((grad_emb, loss))
    grad_z = (inv * (grad_emb - unit * jnp.sum(unit * grad_emb, axis=1, keepdims=True))).astype(BF16)

    g_other = lax.ppermute(grad_z, "zh", SWAP)
    g_near = spread(grad_z, "y", 4).reshape(PART, WIDTH)
    g_far = spread(g_other, "y", 4).reshape(PART, WIDTH)

    def by_zh(rows_of, at):
        return lax.dynamic_index_in_dim(rows_of.reshape(4, 2, ROWS, -1), at, 1, False).reshape(
            PART, -1
        )

    def head_sum(rows_of):
        contract = (((0,), (0,)), ((), ()))
        return lax.dot_general(
            by_zh(rows_of, zh), g_near, contract, preferred_element_type=F32
        ) + lax.dot_general(by_zh(rows_of, 1 - zh), g_far, contract, preferred_element_type=F32)

    features = head.shape[0]
    got = core_swap(head_sum(theirs).astype(BF16)).astype(F32)
    head_part = (head_sum(mine) + got).astype(BF16)
    pieces = head_part.reshape(features, 8, WIDTH // 8).transpose(1, 0, 2)
    head_own = sum_exchange(pieces, XZ).astype(BF16)
    grad_head = spread(head_own, XZ, 8).transpose(1, 0, 2).reshape(features, WIDTH).astype(F32)

    def back(weight):
        contract = (((1,), (1,)), ((), ()))
        near = lax.dot_general(weight, g_near, contract, preferred_element_type=F32).astype(BF16)
        far = lax.dot_general(weight, g_far, contract, preferred_element_type=F32).astype(BF16)
        near, far = near.reshape(features, 4, 1, ROWS), far.reshape(features, 4, 1, ROWS)
        low, high = jnp.where(zh == 0, near, far), jnp.where(zh == 0, far, near)
        return jnp.concatenate([low, high], 2).reshape(features, HALF)

    got = core_swap(back(other_head))
    own = back(head)
    out = jnp.concatenate([jnp.where(core == 0, own, got), jnp.where(core == 0, got, own)], 1)
    return loss, out.T, grad_head


def solution(mesh):
    fine = Mesh(mesh.devices.reshape(4, 2, 4, 2, 2), ("x", "zl", "y", "zh", "c"))
    return jax.shard_map(
        shards,
        mesh=fine,
        in_specs=(P(XZ, CUTS), P(CUTS, None), P(XZ)),
        out_specs=(P(), P(XZ, CUTS), P(CUTS, None)),
        check_vma=False,
    )
```

```python
import jax
import jax.numpy as jnp
from jax import lax
from jax.experimental import pallas as pl
from jax.experimental.pallas import tpu as pltpu
from jax.sharding import Mesh
from jax.sharding import PartitionSpec as P

F32 = jnp.float32
BF16 = jnp.bfloat16
I32 = jnp.int32
SWAP = [(0, 1), (1, 0)]
RING = {s: [(i, (i + s) % 4) for i in range(4)] for s in (1, 2, 3)}
ROWS = 128
PAIR = 256
HALF = 1024
GROUP = 2048
TOTAL = 16384
WIDTH = 1024
VMEM_LIMIT = 40 * 1024 * 1024
YZ, XZ, CUTS = ("y", "zh"), ("x", "zl"), ("y", "zh", "c")
OFFSET = (0, 1, 3, 2)
EXP2_SCALE = 28.853900817779268


def core_swap(value):
    return lax.ppermute(value, "c", SWAP)


def spread(value, axes, count):
    return lax.all_to_all(jnp.broadcast_to(value[None], (count,) + value.shape), axes, 0, 0)


def sum_exchange(parts, axes):
    return jnp.sum(lax.all_to_all(parts, axes, 0, 0).astype(F32), axis=0)


def gather_ring(own, long_axis, short_axis):
    rows = own.shape[0]
    other = lax.ppermute(own, short_axis, SWAP)
    first = lax.axis_index(short_axis) == 0
    pair = jnp.concatenate([jnp.where(first, own, other), jnp.where(first, other, own)], 0)
    after = lax.ppermute(pair, long_axis, RING[3])
    before = lax.ppermute(pair, long_axis, RING[1])
    far_top = lax.ppermute(after[:rows], long_axis, RING[3])
    far_low = lax.ppermute(before[rows:], long_axis, RING[1])
    at = lax.axis_index(long_axis)
    out = jnp.zeros((8 * rows, own.shape[1]), own.dtype)
    for shift, part, skip in (
        (0, pair, 0),
        (1, after, 0),
        (3, before, 0),
        (2, far_top, 0),
        (2, far_low, rows),
    ):
        start = lax.rem(at + shift, 4) * (2 * rows) + skip
        out = lax.dynamic_update_slice_in_dim(out, part, start, 0)
    return out


def chunk_of(start, p, which, own_low):
    return lax.rem(start + OFFSET[p], 4) * 2 + (own_low if which == 0 else 1 - own_low)


def key_column(place, p):
    inner = place[4] * HALF + (place[2] * 2 + place[3]) * ROWS
    near, far = (chunk_of(place[0], p, which, place[1]) * GROUP + inner for which in (0, 1))
    at = lax.broadcasted_iota(I32, (PAIR, 1), 0)
    return at % ROWS + jnp.where(at < ROWS, near, far)


def query_core(place, n):
    return place[4] if n < 4 else 1 - place[4]


def query_chunks(place, n):
    return [
        query_core(place, n) * 8 + chunk_of(place[2], n % 4, which, place[3]) for which in (0, 1)
    ]


def score_kernel(place, *refs):
    key_refs, query_refs = refs[:4], refs[4:12]
    mates, w_ref, row_ref, col_ref, keys, queries, lanes, key_sem, query_sem = refs[12:]
    step = pl.program_id(0)

    def key_copy(p):
        return pltpu.make_async_copy(
            key_refs[p], keys.at[pl.ds(p * PAIR, PAIR), :], key_sem.at[p]
        )

    def query_copy(n):
        return pltpu.make_async_copy(query_refs[n], queries.at[n], query_sem.at[n])

    @pl.when(step == 0)
    def _():
        query_copy(0).start()
        for p in range(4):
            key_copy(p).start()
        for n in range(1, 8):
            query_copy(n).start()
        lanes[...] = jnp.zeros_like(lanes)
        for p in range(4):
            key_copy(p).wait()

    def run(n, masked):
        query_copy(n).wait()
        near, far = query_chunks(place, n)
        mate = jnp.concatenate([mates[near], mates[far]], axis=1)
        col = jnp.zeros((8, PAIR), F32)
        pos = jnp.zeros((8, PAIR), F32)
        for p in range(4):
            at = pl.ds(p * PAIR, PAIR)
            scores = lax.dot_general(
                keys[at, :], queries[n], (((1,), (1,)), ((), ())), preferred_element_type=F32
            )
            kid = key_column(place, p)
            weights = jnp.exp2(scores * EXP2_SCALE)
            if masked and p == 0:
                group = (place[0] * 2 + place[1]) * GROUP
                lane = lax.broadcasted_iota(I32, (1, PAIR), 1)
                qid = group + lane % ROWS + jnp.where(lane < ROWS, near, far) * ROWS
                weights = jnp.where(kid != qid, weights, 0.0)
            w_ref[at, :] = weights
            lanes[at, :] += weights[:, :ROWS] + weights[:, ROWS:]
            hits = jnp.where(kid == mate, scores, 0.0)
            col = col + jnp.sum(weights.reshape(PAIR // 8, 8, PAIR), axis=0)
            pos = pos + jnp.sum(hits.reshape(PAIR // 8, 8, PAIR), axis=0)
        col_ref[near, 0:8, :] = col[:, :ROWS]
        col_ref[far, 0:8, :] = col[:, ROWS:]
        col_ref[near, 8:16, :] = pos[:, :ROWS]
        col_ref[far, 8:16, :] = pos[:, ROWS:]

    for n in range(8):

        @pl.when(step == n)
        def _(n=n):
            run(n, n == 0)

    @pl.when(step == 7)
    def _():
        for p in range(4):
            for which in (0, 1):
                at = pl.ds(p * PAIR + which * ROWS, ROWS)
                row_ref[chunk_of(place[0], p, which, place[1])] = jnp.sum(
                    lanes[at, :], axis=1, keepdims=True
                )


def grad_kernel(place, w_ref, rk_ref, rq_ref, mates, *refs):
    query_refs, (out_ref, queries, query_sem) = refs[:8], refs[8:]
    step = pl.program_id(0)

    def query_copy(n):
        return pltpu.make_async_copy(
            query_refs[n], queries.at[pl.ds(n * PAIR, PAIR), :], query_sem.at[n]
        )

    @pl.when(step == 0)
    def _():
        for n in range(8):
            query_copy(n).start()
        for n in range(8):
            query_copy(n).wait()

    def run(p):
        kid = key_column(place, p)
        near, far = (chunk_of(place[0], p, which, place[1]) for which in (0, 1))
        rk = jnp.concatenate([rk_ref[near], rk_ref[far]], axis=0)
        parts = []
        for n in range(8):
            low, high = query_chunks(place, n)
            rq = jnp.concatenate([rq_ref[low], rq_ref[high]], axis=1)
            mate = jnp.concatenate([mates[low], mates[high]], axis=1)
            grads = w_ref[:, n * PAIR : (n + 1) * PAIR] * (rk + rq)
            parts.append(jnp.where(kid == mate, grads - 40.0, grads).astype(BF16))
        total = jnp.dot(
            jnp.concatenate(parts, axis=1), queries[...], preferred_element_type=F32
        ).astype(BF16)
        out_ref[0, place[1]] = total[:ROWS]
        out_ref[0, 1 - place[1]] = total[ROWS:]

    for p in range(4):

        @pl.when(step == p)
        def _(p=p):
            run(p)


def whole(shape):
    return pl.BlockSpec(shape, lambda t, place: (0,) * len(shape))


def score_call(place, keys, queries, mates):
    return pl.pallas_call(
        score_kernel,
        grid_spec=pltpu.PrefetchScalarGridSpec(
            num_scalar_prefetch=1,
            grid=(8,),
            in_specs=[pl.BlockSpec(memory_space=pl.ANY)] * 12 + [whole((16, 1, ROWS))],
            out_specs=[
                pl.BlockSpec((HALF, PAIR), lambda t, place: (0, t)),
                whole((8, ROWS, 1)),
                whole((16, 16, ROWS)),
            ],
            scratch_shapes=[
                pltpu.VMEM((HALF, WIDTH), BF16),
                pltpu.VMEM((8, PAIR, WIDTH), BF16),
                pltpu.VMEM((HALF, ROWS), F32),
                pltpu.SemaphoreType.DMA((4,)),
                pltpu.SemaphoreType.DMA((8,)),
            ],
        ),
        out_shape=[
            jax.ShapeDtypeStruct((HALF, GROUP), F32),
            jax.ShapeDtypeStruct((8, ROWS, 1), F32),
            jax.ShapeDtypeStruct((16, 16, ROWS), F32),
        ],
        compiler_params=pltpu.CompilerParams(vmem_limit_bytes=VMEM_LIMIT),
        cost_estimate=pl.CostEstimate(
            flops=2 * HALF * GROUP * WIDTH, bytes_accessed=14 << 20, transcendentals=HALF * GROUP
        ),
        name="scores",
    )(place, *keys, *queries, mates)


def grad_call(place, weights, rk, rq, mates, queries):
    return pl.pallas_call(
        grad_kernel,
        grid_spec=pltpu.PrefetchScalarGridSpec(
            num_scalar_prefetch=1,
            grid=(4,),
            in_specs=[
                pl.BlockSpec((PAIR, GROUP), lambda t, place: (t, 0)),
                whole((8, ROWS, 1)),
                whole((16, 1, ROWS)),
                whole((16, 1, ROWS)),
            ]
            + [pl.BlockSpec(memory_space=pl.ANY)] * 8,
            out_specs=pl.BlockSpec(
                (1, 2, ROWS, WIDTH),
                lambda t, place: (
                    lax.rem(place[0] + t + jnp.where(t == 2, 1, 0) - jnp.where(t == 3, 1, 0), 4),
                    0,
                    0,
                    0,
                ),
            ),
            scratch_shapes=[pltpu.VMEM((GROUP, WIDTH), BF16), pltpu.SemaphoreType.DMA((8,))],
        ),
        out_shape=jax.ShapeDtypeStruct((4, 2, ROWS, WIDTH), BF16),
        compiler_params=pltpu.CompilerParams(vmem_limit_bytes=VMEM_LIMIT),
        cost_estimate=pl.CostEstimate(
            flops=2 * HALF * GROUP * WIDTH, bytes_accessed=14 << 20, transcendentals=0
        ),
        name="grads",
    )(place, weights, rk, rq, mates, *queries)


def shards(summaries, head, partner):
    core = lax.axis_index("c")
    place = jnp.stack([lax.axis_index(a) for a in ("x", "zl", "y", "zh", "c")]).astype(I32)
    mates = partner.reshape(16, 1, ROWS)

    mine = lax.dynamic_slice_in_dim(summaries, core * HALF, HALF, 0)
    theirs = core_swap(lax.dynamic_slice_in_dim(summaries, (1 - core) * HALF, HALF, 0))
    other_head = core_swap(head)
    z_part = jnp.dot(mine, head, preferred_element_type=F32) + jnp.dot(
        theirs, other_head, preferred_element_type=F32
    )
    z = sum_exchange(z_part.astype(BF16).reshape(8, ROWS, WIDTH), YZ)
    inv = lax.rsqrt(jnp.sum(z * z, axis=1, keepdims=True) + 1e-06)
    unit = z * inv
    emb = unit.astype(BF16)

    q_pair = jnp.concatenate([emb, lax.ppermute(emb, "zh", SWAP)], 0)
    k_pair = jnp.concatenate([emb, lax.ppermute(emb, "zl", SWAP)], 0)
    queries = [q_pair] + [lax.ppermute(q_pair, "y", RING[4 - s]) for s in OFFSET[1:]]
    keys = [k_pair] + [lax.ppermute(k_pair, "x", RING[4 - s]) for s in OFFSET[1:]]
    queries += [core_swap(a) for a in queries]
    weights, row_part, col_part = score_call(place, keys, queries, mates)

    pos_part = 20.0 * jnp.sum(col_part[:, 8:])
    col_part = jnp.sum(col_part[:, :8], axis=1)
    col_part = jnp.concatenate([col_part, jnp.full((8, ROWS), pos_part, F32)], 0)
    cols = jnp.sum(spread(col_part, CUTS, 16), axis=0)
    rows = jnp.sum(spread(row_part.reshape(8, ROWS), XZ, 8), axis=0)
    den_q, pos = cols[:16], cols[16, 0]
    rk = (20.0 / rows).reshape(8, ROWS, 1)
    rq = (20.0 / den_q).reshape(16, 1, ROWS)
    grad_part = grad_call(place, weights, rk, rq, mates, queries)

    loss = jnp.full((8, 128), jnp.sum(jnp.log(den_q)) - pos, F32)
    loss = jnp.sum(spread(loss, XZ, 8), axis=0)[0, 0] / TOTAL

    grad_emb = sum_exchange(grad_part.reshape(8, ROWS, WIDTH), XZ)
    grad_emb, loss = lax.optimization_barrier((grad_emb, loss))
    grad_z = (inv * (grad_emb - unit * jnp.sum(unit * grad_emb, axis=1, keepdims=True))).astype(BF16)
    grad_half = gather_ring(grad_z, "y", "zh")

    contract_first = (((0,), (0,)), ((), ()))
    head_theirs = lax.dot_general(
        theirs, grad_half, contract_first, preferred_element_type=F32
    ).astype(BF16)
    head_mine = lax.dot_general(mine, grad_half, contract_first, preferred_element_type=F32)
    head_part = (head_mine + core_swap(head_theirs).astype(F32)).astype(BF16)
    features = head.shape[0]
    pieces = head_part.reshape(features, 8, WIDTH // 8).transpose(1, 0, 2)
    head_sum = sum_exchange(pieces, XZ).astype(BF16)
    grad_head = spread(head_sum, XZ, 8).transpose(1, 0, 2).reshape(features, WIDTH).astype(F32)

    contract_last = (((1,), (1,)), ((), ()))
    out_theirs = lax.dot_general(
        other_head, grad_half, contract_last, preferred_element_type=F32
    ).astype(BF16)
    out_mine = lax.dot_general(head, grad_half, contract_last, preferred_element_type=F32).astype(BF16)
    got = core_swap(out_theirs)
    first = core == 0
    out = jnp.concatenate([jnp.where(first, out_mine, got), jnp.where(first, got, out_mine)], 1)
    return loss, out.T, grad_head


def solution(mesh):
    fine = Mesh(mesh.devices.reshape(4, 2, 4, 2, 2), ("x", "zl", "y", "zh", "c"))
    return jax.shard_map(
        shards,
        mesh=fine,
        in_specs=(P(XZ, CUTS), P(CUTS, None), P(XZ)),
        out_specs=(P(), P(XZ, CUTS), P(CUTS, None)),
        check_vma=False,
    )
```

```python
import jax
import jax.numpy as jnp
from jax import lax
from jax.experimental import pallas as pl
from jax.experimental.pallas import tpu as pltpu
from jax.sharding import Mesh
from jax.sharding import PartitionSpec as P

F32 = jnp.float32
BF16 = jnp.bfloat16
I32 = jnp.int32
SWAP = [(0, 1), (1, 0)]
RING = {s: [(i, (i + s) % 4) for i in range(4)] for s in (1, 2, 3)}
ROWS = 128
PAIR = 256
HALF = 1024
GROUP = 2048
TOTAL = 16384
WIDTH = 1024
VMEM_LIMIT = 20 * 1024 * 1024
YZ, XZ, CUTS = ("y", "zh"), ("x", "zl"), ("y", "zh", "c")
OFFSET = (0, 1, 3, 2)
EXP2_SCALE = 28.853900817779268


def core_swap(value):
    return lax.ppermute(value, "c", SWAP)


def spread(value, axes, count):
    return lax.all_to_all(jnp.broadcast_to(value[None], (count,) + value.shape), axes, 0, 0)


def sum_exchange(parts, axes):
    return jnp.sum(lax.all_to_all(parts, axes, 0, 0).astype(F32), axis=0)


def gather_ring(own, long_axis, short_axis):
    rows = own.shape[0]
    pair = jnp.concatenate([own, lax.ppermute(own, short_axis, SWAP)], 0)
    after = lax.ppermute(pair, long_axis, RING[3])
    before = lax.ppermute(pair, long_axis, RING[1])
    far_top = lax.ppermute(after[:rows], long_axis, RING[3])
    far_low = lax.ppermute(before[rows:], long_axis, RING[1])
    return [pair, after, before, far_top, far_low]


def chunk_of(start, p, which, own_low):
    return lax.rem(start + OFFSET[p], 4) * 2 + (own_low if which == 0 else 1 - own_low)


def key_column(place, p):
    inner = place[4] * HALF + (place[2] * 2 + place[3]) * ROWS
    near, far = (chunk_of(place[0], p, which, place[1]) * GROUP + inner for which in (0, 1))
    at = lax.broadcasted_iota(I32, (PAIR, 1), 0)
    return at % ROWS + jnp.where(at < ROWS, near, far)


def query_core(place, n):
    return place[4] if n < 4 else 1 - place[4]


def query_chunks(place, n):
    return [
        query_core(place, n) * 8 + chunk_of(place[2], n % 4, which, place[3]) for which in (0, 1)
    ]


def score_kernel(place, *refs):
    key_refs, query_refs = refs[:5], refs[5:15]
    mates, w_ref, row_ref, col_ref, keys, queries, lanes, sums, key_sem, query_sem = refs[15:]
    step = pl.program_id(0)

    def key_copy(p):
        rows = PAIR if p < 3 else ROWS
        at = p * PAIR if p < 4 else 3 * PAIR + ROWS
        return pltpu.make_async_copy(key_refs[p], keys.at[pl.ds(at, rows), :], key_sem.at[p])

    def query_copies(n):
        first = n // 4 * 5 + n % 4
        if n % 4 < 3:
            return [pltpu.make_async_copy(query_refs[first], queries.at[n], query_sem.at[first])]
        return [
            pltpu.make_async_copy(
                query_refs[first + i],
                queries.at[n, pl.ds(i * ROWS, ROWS), :],
                query_sem.at[first + i],
            )
            for i in (0, 1)
        ]

    @pl.when(step == 0)
    def _():
        for copy in query_copies(0):
            copy.start()
        for p in range(5):
            key_copy(p).start()
        for n in range(1, 8):
            for copy in query_copies(n):
                copy.start()
        lanes[...] = jnp.zeros_like(lanes)
        sums[...] = jnp.zeros_like(sums)
        for p in range(5):
            key_copy(p).wait()

    def run(n, masked):
        for copy in query_copies(n):
            copy.wait()
        near, far = query_chunks(place, n)
        mate = jnp.concatenate([mates[near], mates[far]], axis=1)
        col = jnp.zeros((8, PAIR), F32)
        pos = jnp.zeros((8, PAIR), F32)
        for p in range(4):
            at = pl.ds(p * PAIR, PAIR)
            scores = lax.dot_general(
                keys[at, :], queries[n], (((1,), (1,)), ((), ())), preferred_element_type=F32
            )
            kid = key_column(place, p)
            weights = jnp.exp2(scores * EXP2_SCALE)
            if masked and p == 0:
                group = (place[0] * 2 + place[1]) * GROUP
                lane = lax.broadcasted_iota(I32, (1, PAIR), 1)
                qid = group + lane % ROWS + jnp.where(lane < ROWS, near, far) * ROWS
                weights = jnp.where(kid != qid, weights, 0.0)
            w_ref[at, :] = weights
            lanes[at, :] += weights[:, :ROWS] + weights[:, ROWS:]
            hits = jnp.where(kid == mate, scores, 0.0)
            col = col + jnp.sum(weights.reshape(PAIR // 8, 8, PAIR), axis=0)
            pos = pos + jnp.sum(hits.reshape(PAIR // 8, 8, PAIR), axis=0)
        col = jnp.sum(col, axis=0, keepdims=True)
        sums[pl.ds(near, 1), :] = col[:, :ROWS]
        sums[pl.ds(far, 1), :] = col[:, ROWS:]
        sums[16:24, :] += pos[:, :ROWS] + pos[:, ROWS:]

    for n in range(8):

        @pl.when(step == n)
        def _(n=n):
            run(n, n == 0)

    @pl.when(step == 7)
    def _():
        for device in range(16):
            col_ref[device] = sums[...]
        for p in range(4):
            for which in (0, 1):
                at = pl.ds(p * PAIR + which * ROWS, ROWS)
                row_ref[pl.ds(chunk_of(place[0], p, which, place[1]), 1), :] = jnp.sum(
                    lanes[at, :].T, axis=0, keepdims=True
                )


def grad_kernel(place, w_ref, r0, r1, r2, r3, cols_ref, mates, *refs):
    query_refs, (out_ref, queries, query_sem, rk_ref, rq_ref) = refs[:10], refs[10:]
    step = pl.program_id(0)

    def query_copy(i):
        half, n = i // 5, i % 5
        rows = PAIR if n < 3 else ROWS
        at = half * HALF + (n * PAIR if n < 4 else 3 * PAIR + ROWS)
        return pltpu.make_async_copy(
            query_refs[i], queries.at[pl.ds(at, rows), :], query_sem.at[i]
        )

    @pl.when(step == 0)
    def _():
        for i in range(10):
            query_copy(i).start()
        den = cols_ref[0, 0:16, :]
        for device in range(1, 16):
            den = den + cols_ref[device, 0:16, :]
        rq_ref[...] = 20.0 / den
        rk_ref[...] = 20.0 / (r0[...] + r1[...] + r2[...] + r3[...])
        for i in range(10):
            query_copy(i).wait()

    def column(chunk):
        return jnp.broadcast_to(rk_ref[pl.ds(chunk, 1), :], (ROWS, ROWS)).T

    def run(p):
        kid = key_column(place, p)
        rk = jnp.concatenate(
            [column(chunk_of(place[0], p, which, place[1])) for which in (0, 1)], axis=0
        )
        parts = []
        for n in range(8):
            for which, chunk in enumerate(query_chunks(place, n)):
                start = n * PAIR + which * ROWS
                grads = w_ref[:, start : start + ROWS] * (rk + rq_ref[pl.ds(chunk, 1), :])
                parts.append(jnp.where(kid == mates[chunk], grads - 40.0, grads).astype(BF16))
        total = jnp.dot(
            jnp.concatenate(parts, axis=1), queries[...], preferred_element_type=F32
        ).astype(BF16)
        out_ref[0, place[1]] = total[:ROWS]
        out_ref[0, 1 - place[1]] = total[ROWS:]

    for p in range(4):

        @pl.when(step == p)
        def _(p=p):
            run(p)


def head_kernel(place, mine, theirs, *refs):
    piece_refs, (mine_ref, theirs_ref, all_ref, copy_sem) = refs[:5], refs[5:]
    copies = []
    for p in range(4):
        for which in (0, 1):
            to = pl.multiple_of(chunk_of(place[2], p, which, place[3]) * ROWS, ROWS)
            source = piece_refs[p if p < 3 else 3 + which]
            start = which * ROWS if p < 3 else 0
            copies.append(
                pltpu.make_async_copy(
                    source.at[pl.ds(start, ROWS), :],
                    all_ref.at[pl.ds(to, ROWS), :],
                    copy_sem.at[2 * p + which],
                )
            )
    for copy in copies:
        copy.start()
    for copy in copies:
        copy.wait()
    for source, to in ((theirs, theirs_ref), (mine, mine_ref)):
        total = jnp.dot(source[...], all_ref[...], preferred_element_type=F32).astype(BF16)
        for j in range(8):
            to[j] = total[:, j * ROWS : (j + 1) * ROWS]


def whole(shape):
    return pl.BlockSpec(shape, lambda t, place: (0,) * len(shape))


def score_call(place, keys, queries, mates):
    return pl.pallas_call(
        score_kernel,
        grid_spec=pltpu.PrefetchScalarGridSpec(
            num_scalar_prefetch=1,
            grid=(8,),
            in_specs=[pl.BlockSpec(memory_space=pl.ANY)] * 15 + [whole((16, 1, ROWS))],
            out_specs=[
                pl.BlockSpec((HALF, PAIR), lambda t, place: (0, t)),
                whole((8, ROWS)),
                whole((16, 24, ROWS)),
            ],
            scratch_shapes=[
                pltpu.VMEM((HALF, WIDTH), BF16),
                pltpu.VMEM((8, PAIR, WIDTH), BF16),
                pltpu.VMEM((HALF, ROWS), F32),
                pltpu.VMEM((24, ROWS), F32),
                pltpu.SemaphoreType.DMA((5,)),
                pltpu.SemaphoreType.DMA((10,)),
            ],
        ),
        out_shape=[
            jax.ShapeDtypeStruct((HALF, GROUP), F32),
            jax.ShapeDtypeStruct((8, ROWS), F32),
            jax.ShapeDtypeStruct((16, 24, ROWS), F32),
        ],
        compiler_params=pltpu.CompilerParams(vmem_limit_bytes=VMEM_LIMIT),
        cost_estimate=pl.CostEstimate(
            flops=2 * HALF * GROUP * WIDTH, bytes_accessed=14 << 20, transcendentals=HALF * GROUP
        ),
        name="scores",
    )(place, *keys, *queries, mates)


def grad_call(place, weights, rows, cols, mates, queries):
    return pl.pallas_call(
        grad_kernel,
        grid_spec=pltpu.PrefetchScalarGridSpec(
            num_scalar_prefetch=1,
            grid=(4,),
            in_specs=[pl.BlockSpec((PAIR, GROUP), lambda t, place: (t, 0))]
            + [whole((8, ROWS))] * 4
            + [whole((16, 24, ROWS)), whole((16, 1, ROWS))]
            + [pl.BlockSpec(memory_space=pl.ANY)] * 10,
            out_specs=pl.BlockSpec(
                (1, 2, ROWS, WIDTH),
                lambda t, place: (
                    lax.rem(place[0] + t + jnp.where(t == 2, 1, 0) - jnp.where(t == 3, 1, 0), 4),
                    0,
                    0,
                    0,
                ),
            ),
            scratch_shapes=[
                pltpu.VMEM((GROUP, WIDTH), BF16),
                pltpu.SemaphoreType.DMA((10,)),
                pltpu.VMEM((8, ROWS), F32),
                pltpu.VMEM((16, ROWS), F32),
            ],
        ),
        out_shape=jax.ShapeDtypeStruct((4, 2, ROWS, WIDTH), BF16),
        compiler_params=pltpu.CompilerParams(vmem_limit_bytes=VMEM_LIMIT),
        cost_estimate=pl.CostEstimate(
            flops=2 * HALF * GROUP * WIDTH, bytes_accessed=14 << 20, transcendentals=0
        ),
        name="grads",
    )(place, weights, *rows, cols, mates, *queries)


def head_call(place, mine, theirs, pieces):
    features = mine.shape[0]
    return pl.pallas_call(
        head_kernel,
        grid_spec=pltpu.PrefetchScalarGridSpec(
            num_scalar_prefetch=1,
            grid=(1,),
            in_specs=[whole((features, HALF))] * 2 + [pl.BlockSpec(memory_space=pl.ANY)] * 5,
            out_specs=[whole((8, features, ROWS))] * 2 + [whole((HALF, WIDTH))],
            scratch_shapes=[pltpu.SemaphoreType.DMA((8,))],
        ),
        out_shape=[jax.ShapeDtypeStruct((8, features, ROWS), BF16)] * 2
        + [jax.ShapeDtypeStruct((HALF, WIDTH), BF16)],
        compiler_params=pltpu.CompilerParams(vmem_limit_bytes=VMEM_LIMIT),
        cost_estimate=pl.CostEstimate(
            flops=4 * HALF * features * WIDTH, bytes_accessed=8 << 20, transcendentals=0
        ),
        name="head_parts",
    )(place, mine, theirs, *pieces)


def shards(summaries, head, partner):
    core = lax.axis_index("c")
    place = jnp.stack([lax.axis_index(a) for a in ("x", "zl", "y", "zh", "c")]).astype(I32)
    mates = partner.reshape(16, 1, ROWS)

    turned = summaries.T
    mine = lax.dynamic_slice_in_dim(turned, core * HALF, HALF, 1)
    theirs = core_swap(lax.dynamic_slice_in_dim(turned, (1 - core) * HALF, HALF, 1))
    other_head = core_swap(head)
    first_dims = (((0,), (0,)), ((), ()))
    z_part = lax.dot_general(
        mine, head, first_dims, preferred_element_type=F32
    ) + lax.dot_general(theirs, other_head, first_dims, preferred_element_type=F32)
    z = sum_exchange(z_part.astype(BF16).reshape(8, ROWS, WIDTH), YZ)
    inv = lax.rsqrt(jnp.sum(z * z, axis=1, keepdims=True) + 1e-06)
    unit = z * inv
    emb = unit.astype(BF16)

    keys = gather_ring(emb, "x", "zl")
    queries = gather_ring(emb, "y", "zh")
    queries = queries + [core_swap(piece) for piece in queries]
    weights, row_part, col_part = score_call(place, keys, queries, mates)

    cols = lax.all_to_all(col_part, CUTS, 0, 0)
    row_part = row_part + lax.ppermute(row_part, "zl", SWAP)
    rows = [row_part] + [lax.ppermute(row_part, "x", RING[s]) for s in (1, 3, 2)]
    grad_part = grad_call(place, weights, rows, cols, mates, queries)
    grad_emb = sum_exchange(grad_part.reshape(8, ROWS, WIDTH), XZ)
    grad_z = (inv * (grad_emb - unit * jnp.sum(unit * grad_emb, axis=1, keepdims=True))).astype(BF16)

    head_mine, head_theirs, grad_half = head_call(place, mine, theirs, gather_ring(grad_z, "y", "zh"))
    head_part = head_mine.astype(F32) + core_swap(head_theirs).astype(F32)

    cols = jnp.sum(cols, axis=0)
    loss = jnp.sum(jnp.log(cols[:16])) - 20.0 * jnp.sum(cols[16:])
    terms = []
    for _ in range(3):
        terms.append(lax.reduce_precision(loss, 8, 7))
        loss = loss - terms[-1]
    rider = jnp.stack(terms + [jnp.zeros((), F32)] * 13).astype(BF16)
    rider = jnp.broadcast_to(rider[None, :, None], (8, 16, ROWS))
    pieces = lax.all_to_all(jnp.concatenate([head_part.astype(BF16), rider], 1), XZ, 0, 0)
    pieces = jnp.sum(pieces.astype(F32), axis=0)
    features = head.shape[0]
    loss = jnp.sum(pieces[features:, 0]) / TOTAL
    head_sum = pieces[:features].astype(BF16)
    grad_head = spread(head_sum, XZ, 8).transpose(1, 0, 2).reshape(features, WIDTH).astype(F32)

    last_dims = (((1,), (1,)), ((), ()))
    out_theirs = lax.dot_general(
        other_head, grad_half, last_dims, preferred_element_type=F32
    ).astype(BF16)
    out_mine = lax.dot_general(head, grad_half, last_dims, preferred_element_type=F32).astype(BF16)
    got = core_swap(out_theirs)
    first = core == 0
    out = jnp.concatenate([jnp.where(first, out_mine, got), jnp.where(first, got, out_mine)], 1)
    return loss, out.T, grad_head


def solution(mesh):
    fine = Mesh(mesh.devices.reshape(4, 2, 4, 2, 2), ("x", "zl", "y", "zh", "c"))
    return jax.shard_map(
        shards,
        mesh=fine,
        in_specs=(P(XZ, CUTS), P(CUTS, None), P(XZ)),
        out_specs=(P(), P(XZ, CUTS), P(CUTS, None)),
        check_vma=False,
    )
```

```python
import jax
import jax.numpy as jnp
from jax import lax
from jax.experimental import pallas as pl
from jax.experimental.pallas import tpu as pltpu
from jax.sharding import Mesh
from jax.sharding import PartitionSpec as P

F32 = jnp.float32
BF16 = jnp.bfloat16
I32 = jnp.int32
SWAP = [(0, 1), (1, 0)]
RING = {s: [(i, (i + s) % 4) for i in range(4)] for s in (1, 2, 3)}
ROWS = 128
PAIR = 256
HALF = 1024
GROUP = 2048
TOTAL = 16384
WIDTH = 1024
VMEM_LIMIT = 24 * 1024 * 1024
YZ, XZ, CUTS = ("y", "zh"), ("x", "zl"), ("y", "zh", "c")
OFFSET = (0, 1, 3, 2)
EXP2_SCALE = 28.853900817779268


def core_swap(value):
    return lax.ppermute(value, "c", SWAP)


def spread(value, axes, count):
    return lax.all_to_all(jnp.broadcast_to(value[None], (count,) + value.shape), axes, 0, 0)


def sum_exchange(parts, axes):
    return jnp.sum(lax.all_to_all(parts, axes, 0, 0).astype(F32), axis=0)


def gather_ring(own, long_axis, short_axis):
    other = lax.ppermute(own, short_axis, SWAP)
    after_own = lax.ppermute(own, long_axis, RING[3])
    before_own = lax.ppermute(own, long_axis, RING[1])
    far_own = lax.ppermute(after_own, long_axis, RING[3])
    after_other = lax.ppermute(other, long_axis, RING[3])
    before_other = lax.ppermute(other, long_axis, RING[1])
    far_other = lax.ppermute(before_other, long_axis, RING[1])
    return [own, other, after_own, after_other, before_own, before_other, far_own, far_other]


def chunk_of(start, p, which, own_low):
    return lax.rem(start + OFFSET[p], 4) * 2 + (own_low if which == 0 else 1 - own_low)


def key_column(place, p):
    inner = place[4] * HALF + (place[2] * 2 + place[3]) * ROWS
    near, far = (chunk_of(place[0], p, which, place[1]) * GROUP + inner for which in (0, 1))
    at = lax.broadcasted_iota(I32, (PAIR, 1), 0)
    return at % ROWS + jnp.where(at < ROWS, near, far)


def query_core(place, n):
    return place[4] if n < 4 else 1 - place[4]


def query_chunks(place, n):
    return [
        query_core(place, n) * 8 + chunk_of(place[2], n % 4, which, place[3]) for which in (0, 1)
    ]


def score_kernel(place, *refs):
    key_refs, query_refs = refs[:8], refs[8:24]
    (mates, w_ref, row_ref, col_ref, keys, queries, held, lanes, sums, key_sem, query_sem, out_sem) = refs[24:]
    step = pl.program_id(0)

    def key_copy(i):
        return pltpu.make_async_copy(
            key_refs[i], keys.at[pl.ds(i * ROWS, ROWS), :], key_sem.at[i]
        )

    def query_copies(n):
        return [
            pltpu.make_async_copy(
                query_refs[2 * n + i],
                queries.at[n, pl.ds(i * ROWS, ROWS), :],
                query_sem.at[2 * n + i],
            )
            for i in (0, 1)
        ]

    def out_copy(n):
        return pltpu.make_async_copy(
            held.at[n % 2], w_ref.at[:, pl.ds(n * PAIR, PAIR)], out_sem.at[n % 2]
        )

    @pl.when(step == 0)
    def _():
        for copy in query_copies(0):
            copy.start()
        for i in range(8):
            key_copy(i).start()
        for n in range(1, 8):
            for copy in query_copies(n):
                copy.start()
        lanes[...] = jnp.zeros_like(lanes)
        sums[...] = jnp.zeros_like(sums)
        for i in range(8):
            key_copy(i).wait()

    def run(n, masked):
        for copy in query_copies(n):
            copy.wait()
        if n >= 2:
            out_copy(n - 2).wait()
        near, far = query_chunks(place, n)
        mate = jnp.concatenate([mates[near], mates[far]], axis=1)
        col = jnp.zeros((8, PAIR), F32)
        pos = jnp.zeros((8, PAIR), F32)
        for p in range(4):
            at = pl.ds(p * PAIR, PAIR)
            scores = lax.dot_general(
                keys[at, :], queries[n], (((1,), (1,)), ((), ())), preferred_element_type=F32
            )
            kid = key_column(place, p)
            weights = jnp.exp2(scores * EXP2_SCALE)
            if masked and p == 0:
                group = (place[0] * 2 + place[1]) * GROUP
                lane = lax.broadcasted_iota(I32, (1, PAIR), 1)
                qid = group + lane % ROWS + jnp.where(lane < ROWS, near, far) * ROWS
                weights = jnp.where(kid != qid, weights, 0.0)
            held[n % 2, at, :] = weights
            lanes[at, :] += weights[:, :ROWS] + weights[:, ROWS:]
            hits = jnp.where(kid == mate, scores, 0.0)
            col = col + jnp.sum(weights.reshape(PAIR // 8, 8, PAIR), axis=0)
            pos = pos + jnp.sum(hits.reshape(PAIR // 8, 8, PAIR), axis=0)
        col = jnp.sum(col, axis=0, keepdims=True)
        sums[pl.ds(near, 1), :] = col[:, :ROWS]
        sums[pl.ds(far, 1), :] = col[:, ROWS:]
        sums[16:24, :] += pos[:, :ROWS] + pos[:, ROWS:]
        out_copy(n).start()

    for n in range(8):

        @pl.when(step == n)
        def _(n=n):
            run(n, n == 0)

    @pl.when(step == 7)
    def _():
        for device in range(16):
            col_ref[device] = sums[...]
        for p in range(4):
            for which in (0, 1):
                at = pl.ds(p * PAIR + which * ROWS, ROWS)
                row_ref[pl.ds(chunk_of(place[0], p, which, place[1]), 1), :] = jnp.sum(
                    lanes[at, :].T, axis=0, keepdims=True
                )
        out_copy(6).wait()
        out_copy(7).wait()


def grad_kernel(place, w_ref, r0, r1, r2, r3, cols_ref, mates, *refs):
    query_refs, (out_ref, rider_ref, weights, queries, w_sem, query_sem, rk_ref, rq_ref) = refs[:16], refs[16:]
    step = pl.program_id(0)

    def w_copy(p):
        return pltpu.make_async_copy(
            w_ref.at[pl.ds(p * PAIR, PAIR), :], weights.at[p], w_sem.at[p]
        )

    def query_copy(i):
        return pltpu.make_async_copy(
            query_refs[i], queries.at[pl.ds(i * ROWS, ROWS), :], query_sem.at[i]
        )

    @pl.when(step == 0)
    def _():
        w_copy(0).start()
        for i in range(16):
            query_copy(i).start()
        for p in range(1, 4):
            w_copy(p).start()
        cols = cols_ref[0]
        for device in range(1, 16):
            cols = cols + cols_ref[device]
        den = cols[:16]
        rq_ref[...] = 20.0 / den
        rk_ref[...] = 20.0 / (r0[...] + r1[...] + r2[...] + r3[...])
        logs = jnp.sum(jnp.log(den), axis=0, keepdims=True)
        logs = logs - 20.0 * jnp.sum(cols[16:], axis=0, keepdims=True)
        loss = jnp.broadcast_to(jnp.sum(logs, axis=1, keepdims=True), (16, ROWS))
        row = lax.broadcasted_iota(I32, (16, ROWS), 0)
        rider = jnp.zeros((16, ROWS), F32)
        for i in range(3):
            term = loss.astype(BF16).astype(F32)
            rider = jnp.where(row == i, term, rider)
            loss = loss - term
        rider_ref[...] = rider.astype(BF16)
        for i in range(16):
            query_copy(i).wait()

    def column(chunk):
        return jnp.broadcast_to(rk_ref[pl.ds(chunk, 1), :], (ROWS, ROWS)).T

    def run(p):
        w_copy(p).wait()
        kid = key_column(place, p)
        rk = jnp.concatenate(
            [column(chunk_of(place[0], p, which, place[1])) for which in (0, 1)], axis=0
        )
        parts = []
        for n in range(8):
            for which, chunk in enumerate(query_chunks(place, n)):
                start = n * PAIR + which * ROWS
                grads = weights[p, :, start : start + ROWS] * (rk + rq_ref[pl.ds(chunk, 1), :])
                parts.append(jnp.where(kid == mates[chunk], grads - 40.0, grads).astype(BF16))
        total = jnp.dot(
            jnp.concatenate(parts, axis=1), queries[...], preferred_element_type=F32
        ).astype(BF16)
        out_ref[0, place[1]] = total[:ROWS]
        out_ref[0, 1 - place[1]] = total[ROWS:]

    for p in range(4):

        @pl.when(step == p)
        def _(p=p):
            run(p)


def head_kernel(place, mine, theirs, rider, *refs):
    piece_refs, (mine_ref, theirs_ref, all_ref, copy_sem) = refs[:8], refs[8:]
    features = mine.shape[0]
    copies = []
    for i in range(8):
        to = pl.multiple_of(chunk_of(place[2], i // 2, i % 2, place[3]) * ROWS, ROWS)
        copies.append(
            pltpu.make_async_copy(piece_refs[i], all_ref.at[pl.ds(to, ROWS), :], copy_sem.at[i])
        )
    for copy in copies:
        copy.start()
    for j in range(8):
        mine_ref[j, features:] = rider[...]
        theirs_ref[j, features:] = jnp.zeros_like(rider)
    for copy in copies:
        copy.wait()
    for source, to in ((theirs, theirs_ref), (mine, mine_ref)):
        total = jnp.dot(source[...], all_ref[...], preferred_element_type=F32).astype(BF16)
        for j in range(8):
            to[j, :features] = total[:, j * ROWS : (j + 1) * ROWS]


def whole(shape):
    return pl.BlockSpec(shape, lambda t, place: (0,) * len(shape))


def score_call(place, keys, queries, mates):
    return pl.pallas_call(
        score_kernel,
        grid_spec=pltpu.PrefetchScalarGridSpec(
            num_scalar_prefetch=1,
            grid=(8,),
            in_specs=[pl.BlockSpec(memory_space=pltpu.HBM)] * 24 + [whole((16, 1, ROWS))],
            out_specs=[
                pl.BlockSpec(memory_space=pltpu.HBM),
                whole((8, ROWS)),
                whole((16, 24, ROWS)),
            ],
            scratch_shapes=[
                pltpu.VMEM((HALF, WIDTH), BF16),
                pltpu.VMEM((8, PAIR, WIDTH), BF16),
                pltpu.VMEM((2, HALF, PAIR), F32),
                pltpu.VMEM((HALF, ROWS), F32),
                pltpu.VMEM((24, ROWS), F32),
                pltpu.SemaphoreType.DMA((8,)),
                pltpu.SemaphoreType.DMA((16,)),
                pltpu.SemaphoreType.DMA((2,)),
            ],
        ),
        out_shape=[
            jax.ShapeDtypeStruct((HALF, GROUP), F32),
            jax.ShapeDtypeStruct((8, ROWS), F32),
            jax.ShapeDtypeStruct((16, 24, ROWS), F32),
        ],
        compiler_params=pltpu.CompilerParams(vmem_limit_bytes=VMEM_LIMIT),
        cost_estimate=pl.CostEstimate(
            flops=2 * HALF * GROUP * WIDTH, bytes_accessed=14 << 20, transcendentals=HALF * GROUP
        ),
        name="scores",
    )(place, *keys, *queries, mates)


def grad_call(place, weights, rows, cols, mates, queries):
    return pl.pallas_call(
        grad_kernel,
        grid_spec=pltpu.PrefetchScalarGridSpec(
            num_scalar_prefetch=1,
            grid=(4,),
            in_specs=[pl.BlockSpec(memory_space=pltpu.HBM)]
            + [whole((8, ROWS))] * 4
            + [whole((16, 24, ROWS)), whole((16, 1, ROWS))]
            + [pl.BlockSpec(memory_space=pltpu.HBM)] * 16,
            out_specs=[pl.BlockSpec(
                (1, 2, ROWS, WIDTH),
                lambda t, place: (
                    lax.rem(place[0] + t + jnp.where(t == 2, 1, 0) - jnp.where(t == 3, 1, 0), 4),
                    0,
                    0,
                    0,
                ),
            ), whole((16, ROWS))],
            scratch_shapes=[
                pltpu.VMEM((4, PAIR, GROUP), F32),
                pltpu.VMEM((GROUP, WIDTH), BF16),
                pltpu.SemaphoreType.DMA((4,)),
                pltpu.SemaphoreType.DMA((16,)),
                pltpu.VMEM((8, ROWS), F32),
                pltpu.VMEM((16, ROWS), F32),
            ],
        ),
        out_shape=[
            jax.ShapeDtypeStruct((4, 2, ROWS, WIDTH), BF16),
            jax.ShapeDtypeStruct((16, ROWS), BF16),
        ],
        compiler_params=pltpu.CompilerParams(vmem_limit_bytes=VMEM_LIMIT),
        cost_estimate=pl.CostEstimate(
            flops=2 * HALF * GROUP * WIDTH, bytes_accessed=14 << 20, transcendentals=0
        ),
        name="grads",
    )(place, weights, *rows, cols, mates, *queries)


def head_call(place, mine, theirs, rider, pieces):
    features = mine.shape[0]
    return pl.pallas_call(
        head_kernel,
        grid_spec=pltpu.PrefetchScalarGridSpec(
            num_scalar_prefetch=1,
            grid=(1,),
            in_specs=[whole((features, HALF))] * 2
            + [whole((16, ROWS))]
            + [pl.BlockSpec(memory_space=pltpu.HBM)] * 8,
            out_specs=[whole((8, features + 16, ROWS))] * 2 + [whole((HALF, WIDTH))],
            scratch_shapes=[pltpu.SemaphoreType.DMA((8,))],
        ),
        out_shape=[jax.ShapeDtypeStruct((8, features + 16, ROWS), BF16)] * 2
        + [jax.ShapeDtypeStruct((HALF, WIDTH), BF16)],
        compiler_params=pltpu.CompilerParams(vmem_limit_bytes=VMEM_LIMIT),
        cost_estimate=pl.CostEstimate(
            flops=4 * HALF * features * WIDTH, bytes_accessed=8 << 20, transcendentals=0
        ),
        name="head_parts",
    )(place, mine, theirs, rider, *pieces)


def shards(summaries, head, partner):
    core = lax.axis_index("c")
    place = jnp.stack([lax.axis_index(a) for a in ("x", "zl", "y", "zh", "c")]).astype(I32)
    mates = partner.reshape(16, 1, ROWS)

    turned = summaries.T
    mine = lax.dynamic_slice_in_dim(turned, core * HALF, HALF, 1)
    theirs = core_swap(lax.dynamic_slice_in_dim(turned, (1 - core) * HALF, HALF, 1))
    other_head = core_swap(head)
    first_dims = (((0,), (0,)), ((), ()))
    z_part = lax.dot_general(
        mine, head, first_dims, preferred_element_type=F32
    ) + lax.dot_general(theirs, other_head, first_dims, preferred_element_type=F32)
    z = sum_exchange(z_part.astype(BF16).reshape(8, ROWS, WIDTH), YZ)
    inv = lax.rsqrt(jnp.sum(z * z, axis=1, keepdims=True) + 1e-06)
    unit = z * inv
    emb = unit.astype(BF16)

    keys = gather_ring(emb, "x", "zl")
    queries = gather_ring(emb, "y", "zh")
    queries = queries + [core_swap(piece) for piece in queries]
    weights, row_part, col_part = score_call(place, keys, queries, mates)

    cols = lax.all_to_all(col_part, CUTS, 0, 0)
    row_part = row_part + lax.ppermute(row_part, "zl", SWAP)
    rows = [row_part] + [lax.ppermute(row_part, "x", RING[s]) for s in (1, 3, 2)]
    grad_part, rider = grad_call(place, weights, rows, cols, mates, queries)
    grad_emb = sum_exchange(grad_part.reshape(8, ROWS, WIDTH), XZ)
    grad_z = (inv * (grad_emb - unit * jnp.sum(unit * grad_emb, axis=1, keepdims=True))).astype(BF16)

    head_mine, head_theirs, grad_half = head_call(
        place, mine, theirs, rider, gather_ring(grad_z, "y", "zh")
    )
    head_part = head_mine.astype(F32) + core_swap(head_theirs).astype(F32)

    pieces = lax.all_to_all(head_part.astype(BF16), XZ, 0, 0)
    pieces = jnp.sum(pieces.astype(F32), axis=0)
    features = head.shape[0]
    loss = jnp.sum(pieces[features:, 0]) / TOTAL
    head_sum = pieces[:features].astype(BF16)
    grad_head = spread(head_sum, XZ, 8).transpose(1, 0, 2).reshape(features, WIDTH).astype(F32)

    last_dims = (((1,), (1,)), ((), ()))
    out_theirs = lax.dot_general(
        other_head, grad_half, last_dims, preferred_element_type=F32
    ).astype(BF16)
    out_mine = lax.dot_general(head, grad_half, last_dims, preferred_element_type=F32).astype(BF16)
    got = core_swap(out_theirs)
    first = core == 0
    out = jnp.concatenate([jnp.where(first, out_mine, got), jnp.where(first, got, out_mine)], 1)
    return loss, out.T, grad_head


def solution(mesh):
    fine = Mesh(mesh.devices.reshape(4, 2, 4, 2, 2), ("x", "zl", "y", "zh", "c"))
    return jax.shard_map(
        shards,
        mesh=fine,
        in_specs=(P(XZ, CUTS), P(CUTS, None), P(XZ)),
        out_specs=(P(), P(XZ, CUTS), P(CUTS, None)),
        check_vma=False,
    )
```

```python
import jax
import jax.numpy as jnp
from jax import lax
from jax.experimental import pallas as pl
from jax.experimental.pallas import tpu as pltpu
from jax.sharding import Mesh
from jax.sharding import PartitionSpec as P

F32 = jnp.float32
BF16 = jnp.bfloat16
I32 = jnp.int32
SWAP = [(0, 1), (1, 0)]
RING = {s: [(i, (i + s) % 4) for i in range(4)] for s in (1, 2, 3)}
ROWS = 128
PAIR = 256
HALF = 1024
GROUP = 2048
TOTAL = 16384
WIDTH = 1024
YZ, XZ, CUTS = ("y", "zh"), ("x", "zl"), ("y", "zh", "c")
OFFSET = (0, 1, 3, 2)
EXP2_SCALE = 28.853900817779268


def in_hbm(value):
    return pltpu.with_memory_space_constraint(value, pltpu.HBM)


def core_swap(value):
    return lax.ppermute(value, "c", SWAP)


def spread(value, axes, count):
    return lax.all_to_all(jnp.broadcast_to(value[None], (count,) + value.shape), axes, 0, 0)


def sum_exchange(parts, axes):
    return jnp.sum(lax.all_to_all(parts, axes, 0, 0).astype(F32), axis=0)


def gather_ring(own, long_axis, short_axis):
    other = lax.ppermute(own, short_axis, SWAP)
    after_own = lax.ppermute(own, long_axis, RING[3])
    before_own = lax.ppermute(own, long_axis, RING[1])
    far_own = lax.ppermute(after_own, long_axis, RING[3])
    after_other = lax.ppermute(other, long_axis, RING[3])
    before_other = lax.ppermute(other, long_axis, RING[1])
    far_other = lax.ppermute(before_other, long_axis, RING[1])
    return [own, other, after_own, after_other, before_own, before_other, far_own, far_other]


def chunk_of(start, p, which, own_low):
    return lax.rem(start + OFFSET[p], 4) * 2 + (own_low if which == 0 else 1 - own_low)


def key_column(place, p):
    inner = place[4] * HALF + (place[2] * 2 + place[3]) * ROWS
    near, far = (chunk_of(place[0], p, which, place[1]) * GROUP + inner for which in (0, 1))
    at = lax.broadcasted_iota(I32, (PAIR, 1), 0)
    return at % ROWS + jnp.where(at < ROWS, near, far)


def query_core(place, n):
    return place[4] if n < 4 else 1 - place[4]


def query_chunks(place, n):
    return [
        query_core(place, n) * 8 + chunk_of(place[2], n % 4, which, place[3]) for which in (0, 1)
    ]


def score_kernel(place, *refs):
    key_refs, query_refs = refs[:8], refs[8:24]
    (mates, w_ref, row_ref, col_ref, all_ref) = refs[24:29]
    (keys, queries, held, lanes, sums, key_sem, query_sem, out_sem, all_sem) = refs[29:]
    step = pl.program_id(0)

    def key_copy(i):
        return pltpu.make_async_copy(
            key_refs[i], keys.at[pl.ds(i * ROWS, ROWS), :], key_sem.at[i]
        )

    def query_copies(n):
        return [
            pltpu.make_async_copy(
                query_refs[2 * n + i],
                queries.at[n, pl.ds(i * ROWS, ROWS), :],
                query_sem.at[2 * n + i],
            )
            for i in (0, 1)
        ]

    def all_copy(n):
        return pltpu.make_async_copy(
            queries.at[n], all_ref.at[pl.ds(n * PAIR, PAIR), :], all_sem.at[n]
        )

    def out_copy(n):
        return pltpu.make_async_copy(
            held.at[n % 2], w_ref.at[:, pl.ds(n * PAIR, PAIR)], out_sem.at[n % 2]
        )

    @pl.when(step == 0)
    def _():
        for copy in query_copies(0):
            copy.start()
        for i in range(8):
            key_copy(i).start()
        for n in range(1, 8):
            for copy in query_copies(n):
                copy.start()
        lanes[...] = jnp.zeros_like(lanes)
        sums[...] = jnp.zeros_like(sums)
        for i in range(8):
            key_copy(i).wait()

    def run(n, masked):
        for copy in query_copies(n):
            copy.wait()
        all_copy(n).start()
        if n >= 2:
            out_copy(n - 2).wait()
        near, far = query_chunks(place, n)
        mate = jnp.concatenate([mates[near], mates[far]], axis=1)
        col = jnp.zeros((8, PAIR), F32)
        pos = jnp.zeros((8, PAIR), F32)
        for p in range(4):
            at = pl.ds(p * PAIR, PAIR)
            scores = lax.dot_general(
                keys[at, :], queries[n], (((1,), (1,)), ((), ())), preferred_element_type=F32
            )
            kid = key_column(place, p)
            weights = jnp.exp2(scores * EXP2_SCALE)
            if masked and p == 0:
                group = (place[0] * 2 + place[1]) * GROUP
                lane = lax.broadcasted_iota(I32, (1, PAIR), 1)
                qid = group + lane % ROWS + jnp.where(lane < ROWS, near, far) * ROWS
                weights = jnp.where(kid != qid, weights, 0.0)
            held[n % 2, at, :] = weights
            lanes[at, :] += weights[:, :ROWS] + weights[:, ROWS:]
            hits = jnp.where(kid == mate, scores, 0.0)
            col = col + jnp.sum(weights.reshape(PAIR // 8, 8, PAIR), axis=0)
            pos = pos + jnp.sum(hits.reshape(PAIR // 8, 8, PAIR), axis=0)
        col = jnp.sum(col, axis=0, keepdims=True)
        sums[pl.ds(near, 1), :] = col[:, :ROWS]
        sums[pl.ds(far, 1), :] = col[:, ROWS:]
        sums[16:24, :] += pos[:, :ROWS] + pos[:, ROWS:]
        out_copy(n).start()

    for n in range(8):

        @pl.when(step == n)
        def _(n=n):
            run(n, n == 0)

    @pl.when(step == 7)
    def _():
        for device in range(16):
            col_ref[device] = sums[...]
        for p in range(4):
            for which in (0, 1):
                at = pl.ds(p * PAIR + which * ROWS, ROWS)
                row_ref[pl.ds(chunk_of(place[0], p, which, place[1]), 1), :] = jnp.sum(
                    lanes[at, :].T, axis=0, keepdims=True
                )
        out_copy(6).wait()
        out_copy(7).wait()
        for n in range(8):
            all_copy(n).wait()


def grad_kernel(place, w_ref, query_ref, r0, r1, r2, r3, cols_ref, mates, *refs):
    out_ref, rider_ref, weights, queries, w_sem, query_sem, rk_ref, rq_ref = refs
    step = pl.program_id(0)

    def w_copy(p):
        return pltpu.make_async_copy(
            w_ref.at[pl.ds(p * PAIR, PAIR), :], weights.at[p], w_sem.at[p]
        )

    query_copy = pltpu.make_async_copy(query_ref, queries, query_sem)

    @pl.when(step == 0)
    def _():
        w_copy(0).start()
        query_copy.start()
        for p in range(1, 4):
            w_copy(p).start()
        cols = cols_ref[0]
        for device in range(1, 16):
            cols = cols + cols_ref[device]
        den = cols[:16]
        rq_ref[...] = 20.0 / den
        rk_ref[...] = 20.0 / (r0[...] + r1[...] + r2[...] + r3[...])
        logs = jnp.sum(jnp.log(den), axis=0, keepdims=True)
        logs = logs - 20.0 * jnp.sum(cols[16:], axis=0, keepdims=True)
        loss = jnp.broadcast_to(jnp.sum(logs, axis=1, keepdims=True), (16, ROWS))
        row = lax.broadcasted_iota(I32, (16, ROWS), 0)
        rider = jnp.zeros((16, ROWS), F32)
        for i in range(3):
            term = loss.astype(BF16).astype(F32)
            rider = jnp.where(row == i, term, rider)
            loss = loss - term
        rider_ref[...] = rider.astype(BF16)
        query_copy.wait()

    def column(chunk):
        return jnp.broadcast_to(rk_ref[pl.ds(chunk, 1), :], (ROWS, ROWS)).T

    def run(p):
        w_copy(p).wait()
        kid = key_column(place, p)
        rk = jnp.concatenate(
            [column(chunk_of(place[0], p, which, place[1])) for which in (0, 1)], axis=0
        )
        parts = []
        for n in range(8):
            for which, chunk in enumerate(query_chunks(place, n)):
                start = n * PAIR + which * ROWS
                grads = weights[p, :, start : start + ROWS] * (rk + rq_ref[pl.ds(chunk, 1), :])
                parts.append(jnp.where(kid == mates[chunk], grads - 40.0, grads).astype(BF16))
        total = jnp.dot(
            jnp.concatenate(parts, axis=1), queries[...], preferred_element_type=F32
        ).astype(BF16)
        out_ref[0, place[1]] = total[:ROWS]
        out_ref[0, 1 - place[1]] = total[ROWS:]

    for p in range(4):

        @pl.when(step == p)
        def _(p=p):
            run(p)


def head_kernel(place, mine, theirs, rider, *refs):
    piece_refs, (mine_ref, theirs_ref, all_ref, copy_sem) = refs[:8], refs[8:]
    features = mine.shape[0]
    copies = []
    for i in range(8):
        to = pl.multiple_of(chunk_of(place[2], i // 2, i % 2, place[3]) * ROWS, ROWS)
        copies.append(
            pltpu.make_async_copy(piece_refs[i], all_ref.at[pl.ds(to, ROWS), :], copy_sem.at[i])
        )
    for copy in copies:
        copy.start()
    for j in range(8):
        mine_ref[j, features:] = rider[...]
        theirs_ref[j, features:] = jnp.zeros_like(rider)
    for copy in copies:
        copy.wait()
    for source, to in ((theirs, theirs_ref), (mine, mine_ref)):
        total = jnp.dot(source[...], all_ref[...], preferred_element_type=F32).astype(BF16)
        for j in range(8):
            to[j, :features] = total[:, j * ROWS : (j + 1) * ROWS]


def whole(shape):
    return pl.BlockSpec(shape, lambda t, place: (0,) * len(shape))


def score_call(place, keys, queries, mates):
    return pl.pallas_call(
        score_kernel,
        grid_spec=pltpu.PrefetchScalarGridSpec(
            num_scalar_prefetch=1,
            grid=(8,),
            in_specs=[pl.BlockSpec(memory_space=pl.ANY)] * 24 + [whole((16, 1, ROWS))],
            out_specs=[
                pl.BlockSpec(memory_space=pltpu.HBM),
                whole((8, ROWS)),
                whole((16, 24, ROWS)),
                pl.BlockSpec(memory_space=pltpu.HBM),
            ],
            scratch_shapes=[
                pltpu.VMEM((HALF, WIDTH), BF16),
                pltpu.VMEM((8, PAIR, WIDTH), BF16),
                pltpu.VMEM((2, HALF, PAIR), F32),
                pltpu.VMEM((HALF, ROWS), F32),
                pltpu.VMEM((24, ROWS), F32),
                pltpu.SemaphoreType.DMA((8,)),
                pltpu.SemaphoreType.DMA((16,)),
                pltpu.SemaphoreType.DMA((2,)),
                pltpu.SemaphoreType.DMA((8,)),
            ],
        ),
        out_shape=[
            pltpu.HBM((HALF, GROUP), F32),
            jax.ShapeDtypeStruct((8, ROWS), F32),
            jax.ShapeDtypeStruct((16, 24, ROWS), F32),
            pltpu.HBM((GROUP, WIDTH), BF16),
        ],
        compiler_params=pltpu.CompilerParams(vmem_limit_bytes=12 << 20),
        cost_estimate=pl.CostEstimate(
            flops=2 * HALF * GROUP * WIDTH, bytes_accessed=14 << 20, transcendentals=HALF * GROUP
        ),
        name="scores",
    )(place, *keys, *queries, mates)


def grad_call(place, weights, rows, cols, mates, queries):
    return pl.pallas_call(
        grad_kernel,
        grid_spec=pltpu.PrefetchScalarGridSpec(
            num_scalar_prefetch=1,
            grid=(4,),
            in_specs=[pl.BlockSpec(memory_space=pltpu.HBM)] * 2
            + [whole((8, ROWS))] * 4
            + [whole((16, 24, ROWS)), whole((16, 1, ROWS))],
            out_specs=[pl.BlockSpec(
                (1, 2, ROWS, WIDTH),
                lambda t, place: (
                    lax.rem(place[0] + t + jnp.where(t == 2, 1, 0) - jnp.where(t == 3, 1, 0), 4),
                    0,
                    0,
                    0,
                ),
            ), whole((16, ROWS))],
            scratch_shapes=[
                pltpu.VMEM((4, PAIR, GROUP), F32),
                pltpu.VMEM((GROUP, WIDTH), BF16),
                pltpu.SemaphoreType.DMA((4,)),
                pltpu.SemaphoreType.DMA,
                pltpu.VMEM((8, ROWS), F32),
                pltpu.VMEM((16, ROWS), F32),
            ],
        ),
        out_shape=[
            jax.ShapeDtypeStruct((4, 2, ROWS, WIDTH), BF16),
            jax.ShapeDtypeStruct((16, ROWS), BF16),
        ],
        compiler_params=pltpu.CompilerParams(vmem_limit_bytes=18 << 20),
        cost_estimate=pl.CostEstimate(
            flops=2 * HALF * GROUP * WIDTH, bytes_accessed=14 << 20, transcendentals=0
        ),
        name="grads",
    )(place, in_hbm(weights), in_hbm(queries), *rows, cols, mates)


def head_call(place, mine, theirs, rider, pieces):
    features = mine.shape[0]
    return pl.pallas_call(
        head_kernel,
        grid_spec=pltpu.PrefetchScalarGridSpec(
            num_scalar_prefetch=1,
            grid=(1,),
            in_specs=[whole((features, HALF))] * 2
            + [whole((16, ROWS))]
            + [pl.BlockSpec(memory_space=pl.ANY)] * 8,
            out_specs=[whole((8, features + 16, ROWS))] * 2 + [whole((HALF, WIDTH))],
            scratch_shapes=[pltpu.SemaphoreType.DMA((8,))],
        ),
        out_shape=[jax.ShapeDtypeStruct((8, features + 16, ROWS), BF16)] * 2
        + [pltpu.HBM((HALF, WIDTH), BF16)],
        compiler_params=pltpu.CompilerParams(vmem_limit_bytes=10 << 20),
        cost_estimate=pl.CostEstimate(
            flops=4 * HALF * features * WIDTH, bytes_accessed=8 << 20, transcendentals=0
        ),
        name="head_parts",
    )(place, mine, theirs, rider, *pieces)


def shards(summaries, head, partner):
    core = lax.axis_index("c")
    place = jnp.stack([lax.axis_index(a) for a in ("x", "zl", "y", "zh", "c")]).astype(I32)
    mates = partner.reshape(16, 1, ROWS)

    turned = summaries.T
    mine = lax.dynamic_slice_in_dim(turned, core * HALF, HALF, 1)
    theirs = core_swap(lax.dynamic_slice_in_dim(turned, (1 - core) * HALF, HALF, 1))
    other_head = core_swap(head)
    first_dims = (((0,), (0,)), ((), ()))
    z_part = lax.dot_general(
        mine, head, first_dims, preferred_element_type=F32
    ) + lax.dot_general(theirs, other_head, first_dims, preferred_element_type=F32)
    z_part, place, mates = lax.optimization_barrier((z_part.astype(BF16), place, mates))
    z = sum_exchange(z_part.reshape(8, ROWS, WIDTH), YZ)
    inv = lax.rsqrt(jnp.sum(z * z, axis=1, keepdims=True) + 1e-06)
    unit = z * inv
    emb = unit.astype(BF16)

    keys = gather_ring(emb, "x", "zl")
    queries = gather_ring(emb, "y", "zh")
    queries = queries + [core_swap(piece) for piece in queries]
    weights, row_part, col_part, queries = score_call(place, keys, queries, mates)

    cols = lax.all_to_all(col_part, CUTS, 0, 0)
    row_part = row_part + lax.ppermute(row_part, "zl", SWAP)
    rows = [row_part] + [lax.ppermute(row_part, "x", RING[s]) for s in (1, 3, 2)]
    grad_part, rider = grad_call(place, weights, rows, cols, mates, queries)
    grad_emb = sum_exchange(grad_part.reshape(8, ROWS, WIDTH), XZ)
    grad_z = (inv * (grad_emb - unit * jnp.sum(unit * grad_emb, axis=1, keepdims=True))).astype(BF16)

    head_mine, head_theirs, grad_half = head_call(
        place, mine, theirs, rider, gather_ring(grad_z, "y", "zh")
    )
    head_part = head_mine.astype(F32) + core_swap(head_theirs).astype(F32)

    pieces = lax.all_to_all(head_part.astype(BF16), XZ, 0, 0)
    pieces = jnp.sum(pieces.astype(F32), axis=0)
    features = head.shape[0]
    loss = jnp.sum(pieces[features:, 0]) / TOTAL
    head_sum = pieces[:features].astype(BF16)
    grad_head = spread(head_sum, XZ, 8).transpose(1, 0, 2).reshape(features, WIDTH).astype(F32)

    last_dims = (((1,), (1,)), ((), ()))
    out_theirs = lax.dot_general(
        other_head, grad_half, last_dims, preferred_element_type=F32
    ).astype(BF16)
    out_mine = lax.dot_general(head, grad_half, last_dims, preferred_element_type=F32).astype(BF16)
    got = core_swap(out_theirs)
    first = core == 0
    out = jnp.concatenate([jnp.where(first, out_mine, got), jnp.where(first, got, out_mine)], 1)
    return loss, out.T, grad_head


def solution(mesh):
    fine = Mesh(mesh.devices.reshape(4, 2, 4, 2, 2), ("x", "zl", "y", "zh", "c"))
    return jax.shard_map(
        shards,
        mesh=fine,
        in_specs=(P(XZ, CUTS), P(CUTS, None), P(XZ)),
        out_specs=(P(), P(XZ, CUTS), P(CUTS, None)),
        check_vma=False,
    )
```

```python
import jax
import jax.numpy as jnp
from jax import lax
from jax.experimental import pallas as pl
from jax.experimental.pallas import tpu as pltpu
from jax.sharding import Mesh
from jax.sharding import PartitionSpec as P

F32 = jnp.float32
BF16 = jnp.bfloat16
I32 = jnp.int32
SWAP = [(0, 1), (1, 0)]
RING = {s: [(i, (i + s) % 4) for i in range(4)] for s in (1, 2, 3)}
ROWS = 128
PAIR = 256
HALF = 1024
GROUP = 2048
TOTAL = 16384
WIDTH = 1024
YZ, XZ, CUTS = ("y", "zh"), ("x", "zl"), ("y", "zh", "c")
OFFSET = (0, 1, 3, 2)
EXP2_SCALE = 28.853900817779268


def in_hbm(value):
    return pltpu.with_memory_space_constraint(value, pltpu.HBM)


def core_swap(value):
    return lax.ppermute(value, "c", SWAP)


def spread(value, axes, count):
    return lax.all_to_all(jnp.broadcast_to(value[None], (count,) + value.shape), axes, 0, 0)


def sum_exchange(parts, axes):
    return jnp.sum(lax.all_to_all(parts, axes, 0, 0).astype(F32), axis=0)


def gather_ring(own, long_axis, short_axis):
    other = lax.ppermute(own, short_axis, SWAP)
    after_own = lax.ppermute(own, long_axis, RING[3])
    before_own = lax.ppermute(own, long_axis, RING[1])
    far_own = lax.ppermute(after_own, long_axis, RING[3])
    after_other = lax.ppermute(other, long_axis, RING[3])
    before_other = lax.ppermute(other, long_axis, RING[1])
    far_other = lax.ppermute(before_other, long_axis, RING[1])
    return [own, other, after_own, after_other, before_own, before_other, far_own, far_other]


def chunk_of(start, p, which, own_low):
    return lax.rem(start + OFFSET[p], 4) * 2 + (own_low if which == 0 else 1 - own_low)


def key_column(place, p):
    inner = place[4] * HALF + (place[2] * 2 + place[3]) * ROWS
    near, far = (chunk_of(place[0], p, which, place[1]) * GROUP + inner for which in (0, 1))
    at = lax.broadcasted_iota(I32, (PAIR, 1), 0)
    return at % ROWS + jnp.where(at < ROWS, near, far)


def query_core(place, n):
    return place[4] if n < 4 else 1 - place[4]


def query_chunks(place, n):
    return [
        query_core(place, n) * 8 + chunk_of(place[2], n % 4, which, place[3]) for which in (0, 1)
    ]


def score_kernel(place, *refs):
    key_refs, query_refs = refs[:8], refs[8:24]
    (mates, w_ref, row_ref, col_ref, all_ref) = refs[24:29]
    (keys, queries, held, lanes, sums, key_sem, query_sem, out_sem, all_sem) = refs[29:]
    step = pl.program_id(0)

    def key_copy(i):
        return pltpu.make_async_copy(
            key_refs[i], keys.at[pl.ds(i * ROWS, ROWS), :], key_sem.at[i]
        )

    def query_copies(n):
        return [
            pltpu.make_async_copy(
                query_refs[2 * n + i],
                queries.at[n, pl.ds(i * ROWS, ROWS), :],
                query_sem.at[2 * n + i],
            )
            for i in (0, 1)
        ]

    def all_copy(n):
        return pltpu.make_async_copy(
            queries.at[n], all_ref.at[pl.ds(n * PAIR, PAIR), :], all_sem.at[n]
        )

    def out_copy(n):
        return pltpu.make_async_copy(
            held.at[n % 2], w_ref.at[:, pl.ds(n * PAIR, PAIR)], out_sem.at[n % 2]
        )

    @pl.when(step == 0)
    def _():
        for copy in query_copies(0):
            copy.start()
        for i in range(8):
            key_copy(i).start()
        for n in range(1, 8):
            for copy in query_copies(n):
                copy.start()
        lanes[...] = jnp.zeros_like(lanes)
        sums[...] = jnp.zeros_like(sums)
        for i in range(8):
            key_copy(i).wait()

    def run(n, masked):
        for copy in query_copies(n):
            copy.wait()
        all_copy(n).start()
        if n >= 2:
            out_copy(n - 2).wait()
        near, far = query_chunks(place, n)
        mate = jnp.concatenate([mates[near], mates[far]], axis=1)
        col = jnp.zeros((8, PAIR), F32)
        pos = jnp.zeros((8, PAIR), F32)
        block = lax.dot_general(
            keys[...], queries[n], (((1,), (1,)), ((), ())), preferred_element_type=F32
        )
        for p in range(4):
            at = pl.ds(p * PAIR, PAIR)
            scores = block[p * PAIR : (p + 1) * PAIR]
            kid = key_column(place, p)
            weights = jnp.exp2(scores * EXP2_SCALE)
            if masked and p == 0:
                group = (place[0] * 2 + place[1]) * GROUP
                lane = lax.broadcasted_iota(I32, (1, PAIR), 1)
                qid = group + lane % ROWS + jnp.where(lane < ROWS, near, far) * ROWS
                weights = jnp.where(kid != qid, weights, 0.0)
            held[n % 2, at, :] = weights
            lanes[at, :] += weights[:, :ROWS] + weights[:, ROWS:]
            hits = jnp.where(kid == mate, scores, 0.0)
            col = col + jnp.sum(weights.reshape(PAIR // 8, 8, PAIR), axis=0)
            pos = pos + jnp.sum(hits.reshape(PAIR // 8, 8, PAIR), axis=0)
        col = jnp.sum(col, axis=0, keepdims=True)
        sums[pl.ds(near, 1), :] = col[:, :ROWS]
        sums[pl.ds(far, 1), :] = col[:, ROWS:]
        sums[16:24, :] += pos[:, :ROWS] + pos[:, ROWS:]
        out_copy(n).start()

    for n in range(8):

        @pl.when(step == n)
        def _(n=n):
            run(n, n == 0)

    @pl.when(step == 7)
    def _():
        for device in range(16):
            col_ref[device] = sums[...]
        for p in range(4):
            for which in (0, 1):
                at = pl.ds(p * PAIR + which * ROWS, ROWS)
                row_ref[pl.ds(chunk_of(place[0], p, which, place[1]), 1), :] = jnp.sum(
                    lanes[at, :].T, axis=0, keepdims=True
                )
        out_copy(6).wait()
        out_copy(7).wait()
        for n in range(8):
            all_copy(n).wait()


def grad_kernel(place, w_ref, query_ref, r0, r1, r2, r3, cols_ref, mates, *refs):
    out_ref, rider_ref, weights, queries, w_sem, query_sem, rk_ref, rq_ref = refs
    step = pl.program_id(0)

    def w_copy(p):
        return pltpu.make_async_copy(
            w_ref.at[pl.ds(p * PAIR, PAIR), :], weights.at[p], w_sem.at[p]
        )

    query_copy = pltpu.make_async_copy(query_ref, queries, query_sem)

    @pl.when(step == 0)
    def _():
        w_copy(0).start()
        query_copy.start()
        for p in range(1, 4):
            w_copy(p).start()
        cols = cols_ref[0]
        for device in range(1, 16):
            cols = cols + cols_ref[device]
        den = cols[:16]
        rq_ref[...] = 20.0 / den
        rk_ref[...] = 20.0 / (r0[...] + r1[...] + r2[...] + r3[...])
        logs = jnp.sum(jnp.log(den), axis=0, keepdims=True)
        logs = logs - 20.0 * jnp.sum(cols[16:], axis=0, keepdims=True)
        loss = jnp.broadcast_to(jnp.sum(logs, axis=1, keepdims=True), (16, ROWS))
        row = lax.broadcasted_iota(I32, (16, ROWS), 0)
        rider = jnp.zeros((16, ROWS), F32)
        for i in range(3):
            term = loss.astype(BF16).astype(F32)
            rider = jnp.where(row == i, term, rider)
            loss = loss - term
        rider_ref[...] = rider.astype(BF16)
        query_copy.wait()

    def column(chunk):
        return jnp.broadcast_to(rk_ref[pl.ds(chunk, 1), :], (ROWS, ROWS)).T

    def run(p):
        w_copy(p).wait()
        kid = key_column(place, p)
        rk = jnp.concatenate(
            [column(chunk_of(place[0], p, which, place[1])) for which in (0, 1)], axis=0
        )
        parts = []
        for n in range(8):
            for which, chunk in enumerate(query_chunks(place, n)):
                start = n * PAIR + which * ROWS
                grads = weights[p, :, start : start + ROWS] * (rk + rq_ref[pl.ds(chunk, 1), :])
                parts.append(jnp.where(kid == mates[chunk], grads - 40.0, grads).astype(BF16))
        total = jnp.dot(
            jnp.concatenate(parts, axis=1), queries[...], preferred_element_type=F32
        ).astype(BF16)
        out_ref[0, place[1]] = total[:ROWS]
        out_ref[0, 1 - place[1]] = total[ROWS:]

    for p in range(4):

        @pl.when(step == p)
        def _(p=p):
            run(p)


def head_kernel(place, summaries, rider, *refs):
    piece_refs, (head_ref, all_ref, rows, copy_sem, out_sem) = refs[:16], refs[16:]
    features = summaries.shape[0]
    copies = []
    for n in range(8):
        for i, chunk in enumerate(query_chunks(place, n)):
            to = pl.multiple_of(chunk * ROWS, ROWS)
            at = 2 * n + i
            copies.append(
                pltpu.make_async_copy(
                    piece_refs[at], rows.at[pl.ds(to, ROWS), :], copy_sem.at[at]
                )
            )
    for copy in copies:
        copy.start()
    for j in range(8):
        head_ref[j, features:] = rider[...]
    for copy in copies:
        copy.wait()
    out = pltpu.make_async_copy(rows, all_ref, out_sem)
    out.start()
    total = jnp.dot(summaries[...], rows[...], preferred_element_type=F32).astype(BF16)
    for j in range(8):
        head_ref[j, :features] = total[:, j * ROWS : (j + 1) * ROWS]
    out.wait()


def whole(shape):
    return pl.BlockSpec(shape, lambda t, place: (0,) * len(shape))


def score_call(place, keys, queries, mates):
    return pl.pallas_call(
        score_kernel,
        grid_spec=pltpu.PrefetchScalarGridSpec(
            num_scalar_prefetch=1,
            grid=(8,),
            in_specs=[pl.BlockSpec(memory_space=pl.ANY)] * 24 + [whole((16, 1, ROWS))],
            out_specs=[
                pl.BlockSpec(memory_space=pltpu.HBM),
                whole((8, ROWS)),
                whole((16, 24, ROWS)),
                pl.BlockSpec(memory_space=pltpu.HBM),
            ],
            scratch_shapes=[
                pltpu.VMEM((HALF, WIDTH), BF16),
                pltpu.VMEM((8, PAIR, WIDTH), BF16),
                pltpu.VMEM((2, HALF, PAIR), F32),
                pltpu.VMEM((HALF, ROWS), F32),
                pltpu.VMEM((24, ROWS), F32),
                pltpu.SemaphoreType.DMA((8,)),
                pltpu.SemaphoreType.DMA((16,)),
                pltpu.SemaphoreType.DMA((2,)),
                pltpu.SemaphoreType.DMA((8,)),
            ],
        ),
        out_shape=[
            pltpu.HBM((HALF, GROUP), F32),
            jax.ShapeDtypeStruct((8, ROWS), F32),
            jax.ShapeDtypeStruct((16, 24, ROWS), F32),
            pltpu.HBM((GROUP, WIDTH), BF16),
        ],
        compiler_params=pltpu.CompilerParams(vmem_limit_bytes=12 << 20),
        cost_estimate=pl.CostEstimate(
            flops=2 * HALF * GROUP * WIDTH, bytes_accessed=14 << 20, transcendentals=HALF * GROUP
        ),
        name="scores",
    )(place, *keys, *queries, mates)


def grad_call(place, weights, rows, cols, mates, queries):
    return pl.pallas_call(
        grad_kernel,
        grid_spec=pltpu.PrefetchScalarGridSpec(
            num_scalar_prefetch=1,
            grid=(4,),
            in_specs=[pl.BlockSpec(memory_space=pltpu.HBM)] * 2
            + [whole((8, ROWS))] * 4
            + [whole((16, 24, ROWS)), whole((16, 1, ROWS))],
            out_specs=[pl.BlockSpec(
                (1, 2, ROWS, WIDTH),
                lambda t, place: (
                    lax.rem(place[0] + t + jnp.where(t == 2, 1, 0) - jnp.where(t == 3, 1, 0), 4),
                    0,
                    0,
                    0,
                ),
            ), whole((16, ROWS))],
            scratch_shapes=[
                pltpu.VMEM((4, PAIR, GROUP), F32),
                pltpu.VMEM((GROUP, WIDTH), BF16),
                pltpu.SemaphoreType.DMA((4,)),
                pltpu.SemaphoreType.DMA,
                pltpu.VMEM((8, ROWS), F32),
                pltpu.VMEM((16, ROWS), F32),
            ],
        ),
        out_shape=[
            jax.ShapeDtypeStruct((4, 2, ROWS, WIDTH), BF16),
            jax.ShapeDtypeStruct((16, ROWS), BF16),
        ],
        compiler_params=pltpu.CompilerParams(vmem_limit_bytes=18 << 20),
        cost_estimate=pl.CostEstimate(
            flops=2 * HALF * GROUP * WIDTH, bytes_accessed=14 << 20, transcendentals=0
        ),
        name="grads",
    )(place, in_hbm(weights), in_hbm(queries), *rows, cols, mates)


def head_call(place, summaries, rider, pieces):
    features = summaries.shape[0]
    return pl.pallas_call(
        head_kernel,
        grid_spec=pltpu.PrefetchScalarGridSpec(
            num_scalar_prefetch=1,
            grid=(1,),
            in_specs=[whole((features, GROUP)), whole((16, ROWS))]
            + [pl.BlockSpec(memory_space=pl.ANY)] * 16,
            out_specs=[whole((8, features + 16, ROWS)), pl.BlockSpec(memory_space=pltpu.HBM)],
            scratch_shapes=[
                pltpu.VMEM((GROUP, WIDTH), BF16),
                pltpu.SemaphoreType.DMA((16,)),
                pltpu.SemaphoreType.DMA,
            ],
        ),
        out_shape=[
            jax.ShapeDtypeStruct((8, features + 16, ROWS), BF16),
            pltpu.HBM((GROUP, WIDTH), BF16),
        ],
        compiler_params=pltpu.CompilerParams(vmem_limit_bytes=20 << 20),
        cost_estimate=pl.CostEstimate(
            flops=2 * GROUP * features * WIDTH, bytes_accessed=10 << 20, transcendentals=0
        ),
        name="head_parts",
    )(place, summaries, rider, *pieces)


def shards(summaries, head, partner):
    core = lax.axis_index("c")
    place = jnp.stack([lax.axis_index(a) for a in ("x", "zl", "y", "zh", "c")]).astype(I32)
    mates = partner.reshape(16, 1, ROWS)

    turned = summaries.T
    mine = lax.dynamic_slice_in_dim(turned, core * HALF, HALF, 1)
    theirs = core_swap(lax.dynamic_slice_in_dim(turned, (1 - core) * HALF, HALF, 1))
    other_head = core_swap(head)
    first_dims = (((0,), (0,)), ((), ()))
    z_part = lax.dot_general(
        mine, head, first_dims, preferred_element_type=F32
    ) + lax.dot_general(theirs, other_head, first_dims, preferred_element_type=F32)
    z_part, place, mates = lax.optimization_barrier((z_part.astype(BF16), place, mates))
    z = sum_exchange(z_part.reshape(8, ROWS, WIDTH), YZ)
    inv = lax.rsqrt(jnp.sum(z * z, axis=1, keepdims=True) + 1e-06)
    unit = z * inv
    emb = unit.astype(BF16)

    keys = gather_ring(emb, "x", "zl")
    queries = gather_ring(emb, "y", "zh")
    queries = queries + [core_swap(piece) for piece in queries]
    weights, row_part, col_part, queries = score_call(place, keys, queries, mates)

    cols = lax.all_to_all(col_part, CUTS, 0, 0)
    row_part = row_part + lax.ppermute(row_part, "zl", SWAP)
    rows = [row_part] + [lax.ppermute(row_part, "x", RING[s]) for s in (1, 3, 2)]
    grad_part, rider = grad_call(place, weights, rows, cols, mates, queries)
    grad_emb = sum_exchange(grad_part.reshape(8, ROWS, WIDTH), XZ)
    grad_z = (inv * (grad_emb - unit * jnp.sum(unit * grad_emb, axis=1, keepdims=True))).astype(BF16)

    pieces = gather_ring(grad_z, "y", "zh")
    pieces = pieces + [core_swap(piece) for piece in pieces]
    head_part, grad_group = head_call(place, turned, rider, pieces)
    pieces = lax.all_to_all(head_part, XZ, 0, 0)
    pieces = jnp.sum(pieces.astype(F32), axis=0)
    features = head.shape[0]
    loss = jnp.sum(pieces[features:, 0]) / TOTAL
    head_sum = pieces[:features].astype(BF16)
    grad_head = spread(head_sum, XZ, 8).transpose(1, 0, 2).reshape(features, WIDTH).astype(F32)

    last_dims = (((1,), (1,)), ((), ()))
    out = lax.dot_general(head, grad_group, last_dims, preferred_element_type=F32).astype(BF16)
    return loss, out.T, grad_head


def solution(mesh):
    fine = Mesh(mesh.devices.reshape(4, 2, 4, 2, 2), ("x", "zl", "y", "zh", "c"))
    return jax.shard_map(
        shards,
        mesh=fine,
        in_specs=(P(XZ, CUTS), P(CUTS, None), P(XZ)),
        out_specs=(P(), P(XZ, CUTS), P(CUTS, None)),
        check_vma=False,
    )
```

```python
import jax
import jax.numpy as jnp
from jax import lax
from jax.experimental import pallas as pl
from jax.experimental.pallas import tpu as pltpu
from jax.sharding import Mesh
from jax.sharding import PartitionSpec as P

F32 = jnp.float32
BF16 = jnp.bfloat16
I32 = jnp.int32
SWAP = [(0, 1), (1, 0)]
RING = {s: [(i, (i + s) % 4) for i in range(4)] for s in (1, 2, 3)}
ROWS = 128
PAIR = 256
HALF = 1024
GROUP = 2048
TOTAL = 16384
WIDTH = 1024
YZ, XZ, CUTS = ("y", "zh"), ("x", "zl"), ("y", "zh", "c")
OFFSET = (0, 1, 3, 2)
EXP2_SCALE = 28.853900817779268


def in_hbm(value):
    return pltpu.with_memory_space_constraint(value, pltpu.HBM)


def core_swap(value):
    return lax.ppermute(value, "c", SWAP)


def spread(value, axes, count):
    return lax.all_to_all(jnp.broadcast_to(value[None], (count,) + value.shape), axes, 0, 0)


def sum_exchange(parts, axes):
    return jnp.sum(lax.all_to_all(parts, axes, 0, 0).astype(F32), axis=0)


def gather_ring(own, long_axis, short_axis):
    other = lax.ppermute(own, short_axis, SWAP)
    after_own = lax.ppermute(own, long_axis, RING[3])
    before_own = lax.ppermute(own, long_axis, RING[1])
    far_own = lax.ppermute(after_own, long_axis, RING[3])
    after_other = lax.ppermute(other, long_axis, RING[3])
    before_other = lax.ppermute(other, long_axis, RING[1])
    far_other = lax.ppermute(before_other, long_axis, RING[1])
    return [own, other, after_own, after_other, before_own, before_other, far_own, far_other]


def chunk_of(start, p, which, own_low):
    return lax.rem(start + OFFSET[p], 4) * 2 + (own_low if which == 0 else 1 - own_low)


def key_column(place, p):
    inner = place[4] * HALF + (place[2] * 2 + place[3]) * ROWS
    near, far = (chunk_of(place[0], p, which, place[1]) * GROUP + inner for which in (0, 1))
    at = lax.broadcasted_iota(I32, (PAIR, 1), 0)
    return at % ROWS + jnp.where(at < ROWS, near, far)


def query_core(place, n):
    return place[4] if n < 4 else 1 - place[4]


def query_chunks(place, n):
    return [
        query_core(place, n) * 8 + chunk_of(place[2], n % 4, which, place[3]) for which in (0, 1)
    ]


def score_kernel(place, *refs):
    key_refs, query_refs = refs[:8], refs[8:24]
    (mates, w_ref, row_ref, hit_ref, col_ref, all_ref) = refs[24:30]
    (keys, queries, held, lanes, hit_lanes, sums, key_sem, query_sem, out_sem, all_sem) = refs[30:]
    step = pl.program_id(0)

    def key_copy(i):
        return pltpu.make_async_copy(
            key_refs[i], keys.at[pl.ds(i * ROWS, ROWS), :], key_sem.at[i]
        )

    def query_copies(n):
        return [
            pltpu.make_async_copy(
                query_refs[2 * n + i],
                queries.at[n, pl.ds(i * ROWS, ROWS), :],
                query_sem.at[2 * n + i],
            )
            for i in (0, 1)
        ]

    def all_copy(n):
        return pltpu.make_async_copy(
            queries.at[n], all_ref.at[pl.ds(n * PAIR, PAIR), :], all_sem.at[n]
        )

    def out_copy(n):
        return pltpu.make_async_copy(
            held.at[n % 2], w_ref.at[:, pl.ds(n * PAIR, PAIR)], out_sem.at[n % 2]
        )

    @pl.when(step == 0)
    def _():
        for copy in query_copies(0):
            copy.start()
        for i in range(8):
            key_copy(i).start()
        for n in range(1, 8):
            for copy in query_copies(n):
                copy.start()
        lanes[...] = jnp.zeros_like(lanes)
        hit_lanes[...] = jnp.zeros_like(hit_lanes)
        for i in range(8):
            key_copy(i).wait()

    def run(n, masked):
        for copy in query_copies(n):
            copy.wait()
        all_copy(n).start()
        if n >= 2:
            out_copy(n - 2).wait()
        near, far = query_chunks(place, n)
        mate = jnp.concatenate([mates[near], mates[far]], axis=1)
        col = jnp.zeros((8, PAIR), F32)
        block = lax.dot_general(
            keys[...], queries[n], (((1,), (1,)), ((), ())), preferred_element_type=F32
        )
        for p in range(4):
            at = pl.ds(p * PAIR, PAIR)
            scores = block[p * PAIR : (p + 1) * PAIR]
            kid = key_column(place, p)
            weights = jnp.exp2(scores * EXP2_SCALE)
            if masked and p == 0:
                group = (place[0] * 2 + place[1]) * GROUP
                lane = lax.broadcasted_iota(I32, (1, PAIR), 1)
                qid = group + lane % ROWS + jnp.where(lane < ROWS, near, far) * ROWS
                weights = jnp.where(kid != qid, weights, 0.0)
            held[n % 2, at, :] = weights.astype(BF16)
            lanes[at, :] += weights[:, :ROWS] + weights[:, ROWS:]
            hits = jnp.where(kid == mate, weights, 0.0)
            hit_lanes[at, :] += hits[:, :ROWS] + hits[:, ROWS:]
            col = col + jnp.sum(weights.reshape(PAIR // 8, 8, PAIR), axis=0)
        col = jnp.sum(col, axis=0, keepdims=True)
        sums[pl.ds(near, 1), :] = col[:, :ROWS]
        sums[pl.ds(far, 1), :] = col[:, ROWS:]
        out_copy(n).start()

    for n in range(8):

        @pl.when(step == n)
        def _(n=n):
            run(n, n == 0)

    @pl.when(step == 7)
    def _():
        for p in range(4):
            for which in (0, 1):
                at = pl.ds(p * PAIR + which * ROWS, ROWS)
                chunk = chunk_of(place[0], p, which, place[1])
                hits = jnp.sum(hit_lanes[at, :].T, axis=0, keepdims=True)
                hit_ref[pl.ds(chunk, 1), :] = hits
                row_ref[pl.ds(chunk, 1), :] = jnp.sum(lanes[at, :].T, axis=0, keepdims=True)
                found = hits > 0.0
                sums[16 + 2 * p + which : 17 + 2 * p + which, :] = jnp.where(
                    found, jnp.log(jnp.where(found, hits, 1.0)), 0.0
                )
        for device in range(16):
            col_ref[device] = sums[...]
        out_copy(6).wait()
        out_copy(7).wait()
        for n in range(8):
            all_copy(n).wait()


def grad_kernel(place, w_ref, query_ref, hit_ref, r0, r1, r2, r3, cols_ref, mates, *refs):
    out_ref, rider_ref, weights, queries, w_sem, query_sem, rk_ref, rq_ref = refs

    def w_copy(p):
        return pltpu.make_async_copy(
            w_ref.at[pl.ds(p * PAIR, PAIR), :], weights.at[p], w_sem.at[p]
        )

    query_copy = pltpu.make_async_copy(query_ref, queries, query_sem)

    w_copy(0).start()
    query_copy.start()
    for p in range(1, 4):
        w_copy(p).start()
    cols = cols_ref[0]
    for device in range(1, 16):
        cols = cols + cols_ref[device]
    den = cols[:16]
    rq_ref[...] = 20.0 / den
    rk_ref[...] = 20.0 / (r0[...] + r1[...] + r2[...] + r3[...])
    logs = jnp.sum(jnp.log(den), axis=0, keepdims=True)
    logs = logs - jnp.sum(cols[16:], axis=0, keepdims=True)
    loss = jnp.broadcast_to(jnp.sum(logs, axis=1, keepdims=True), (16, ROWS))
    row = lax.broadcasted_iota(I32, (16, ROWS), 0)
    rider = jnp.zeros((16, ROWS), F32)
    for i in range(3):
        term = loss.astype(BF16).astype(F32)
        rider = jnp.where(row == i, term, rider)
        loss = loss - term
    rider_ref[...] = rider.astype(BF16)

    def columns(source, p):
        chunks = [chunk_of(place[0], p, which, place[1]) for which in (0, 1)]
        return jnp.concatenate(
            [jnp.broadcast_to(source[pl.ds(chunk, 1), :], (ROWS, ROWS)).T for chunk in chunks], axis=0
        )

    def run(p):
        w_copy(p).wait()
        kid = key_column(place, p)
        rk, hit_weights = columns(rk_ref, p), columns(hit_ref, p)
        parts = []
        for n in range(8):
            for which, chunk in enumerate(query_chunks(place, n)):
                start = n * PAIR + which * ROWS
                hit = kid == mates[chunk]
                chosen = jnp.where(hit, hit_weights, weights[p, :, start : start + ROWS].astype(F32))
                grads = chosen * (rk + rq_ref[pl.ds(chunk, 1), :])
                parts.append(jnp.where(hit, grads - 40.0, grads).astype(BF16))
        if p == 0:
            query_copy.wait()
        total = jnp.dot(
            jnp.concatenate(parts, axis=1), queries[...], preferred_element_type=F32
        ).astype(BF16)
        at = lax.rem(place[0] + OFFSET[p], 4)
        out_ref[at, place[1]] = total[:ROWS]
        out_ref[at, 1 - place[1]] = total[ROWS:]

    for p in range(4):
        run(p)


def head_kernel(place, summaries, rider, *refs):
    piece_refs, (head_ref, all_ref, rows, copy_sem, out_sem) = refs[:16], refs[16:]
    features = summaries.shape[0]
    copies = []
    for n in range(8):
        for i, chunk in enumerate(query_chunks(place, n)):
            to = pl.multiple_of(chunk * ROWS, ROWS)
            at = 2 * n + i
            copies.append(
                pltpu.make_async_copy(
                    piece_refs[at], rows.at[pl.ds(to, ROWS), :], copy_sem.at[at]
                )
            )
    for copy in copies:
        copy.start()
    for j in range(8):
        head_ref[j, features:] = rider[...]
    for copy in copies:
        copy.wait()
    out = pltpu.make_async_copy(rows, all_ref, out_sem)
    out.start()
    total = jnp.dot(summaries[...], rows[...], preferred_element_type=F32).astype(BF16)
    for j in range(8):
        head_ref[j, :features] = total[:, j * ROWS : (j + 1) * ROWS]
    out.wait()


def whole(shape):
    return pl.BlockSpec(shape, lambda t, place: (0,) * len(shape))


def score_call(place, keys, queries, mates):
    return pl.pallas_call(
        score_kernel,
        grid_spec=pltpu.PrefetchScalarGridSpec(
            num_scalar_prefetch=1,
            grid=(8,),
            in_specs=[pl.BlockSpec(memory_space=pl.ANY)] * 24 + [whole((16, 1, ROWS))],
            out_specs=[
                pl.BlockSpec(memory_space=pltpu.HBM),
                whole((8, ROWS)),
                whole((8, ROWS)),
                whole((16, 24, ROWS)),
                pl.BlockSpec(memory_space=pltpu.HBM),
            ],
            scratch_shapes=[
                pltpu.VMEM((HALF, WIDTH), BF16),
                pltpu.VMEM((8, PAIR, WIDTH), BF16),
                pltpu.VMEM((2, HALF, PAIR), BF16),
                pltpu.VMEM((HALF, ROWS), F32),
                pltpu.VMEM((HALF, ROWS), F32),
                pltpu.VMEM((24, ROWS), F32),
                pltpu.SemaphoreType.DMA((8,)),
                pltpu.SemaphoreType.DMA((16,)),
                pltpu.SemaphoreType.DMA((2,)),
                pltpu.SemaphoreType.DMA((8,)),
            ],
        ),
        out_shape=[
            pltpu.HBM((HALF, GROUP), BF16),
            jax.ShapeDtypeStruct((8, ROWS), F32),
            jax.ShapeDtypeStruct((8, ROWS), F32),
            jax.ShapeDtypeStruct((16, 24, ROWS), F32),
            pltpu.HBM((GROUP, WIDTH), BF16),
        ],
        compiler_params=pltpu.CompilerParams(vmem_limit_bytes=12 << 20),
        cost_estimate=pl.CostEstimate(
            flops=2 * HALF * GROUP * WIDTH, bytes_accessed=14 << 20, transcendentals=HALF * GROUP
        ),
        name="scores",
    )(place, *keys, *queries, mates)


def grad_call(place, weights, hits, rows, cols, mates, queries):
    return pl.pallas_call(
        grad_kernel,
        grid_spec=pltpu.PrefetchScalarGridSpec(
            num_scalar_prefetch=1,
            grid=(1,),
            in_specs=[pl.BlockSpec(memory_space=pltpu.HBM)] * 2
            + [whole((8, ROWS))] * 5
            + [whole((16, 24, ROWS)), whole((16, 1, ROWS))],
            out_specs=[whole((4, 2, ROWS, WIDTH)), whole((16, ROWS))],
            scratch_shapes=[
                pltpu.VMEM((4, PAIR, GROUP), BF16),
                pltpu.VMEM((GROUP, WIDTH), BF16),
                pltpu.SemaphoreType.DMA((4,)),
                pltpu.SemaphoreType.DMA,
                pltpu.VMEM((8, ROWS), F32),
                pltpu.VMEM((16, ROWS), F32),
            ],
        ),
        out_shape=[
            jax.ShapeDtypeStruct((4, 2, ROWS, WIDTH), BF16),
            jax.ShapeDtypeStruct((16, ROWS), BF16),
        ],
        compiler_params=pltpu.CompilerParams(vmem_limit_bytes=18 << 20),
        cost_estimate=pl.CostEstimate(
            flops=2 * HALF * GROUP * WIDTH, bytes_accessed=14 << 20, transcendentals=0
        ),
        name="grads",
    )(place, in_hbm(weights), in_hbm(queries), hits, *rows, cols, mates)


def head_call(place, summaries, rider, pieces):
    features = summaries.shape[0]
    return pl.pallas_call(
        head_kernel,
        grid_spec=pltpu.PrefetchScalarGridSpec(
            num_scalar_prefetch=1,
            grid=(1,),
            in_specs=[whole((features, GROUP)), whole((16, ROWS))]
            + [pl.BlockSpec(memory_space=pl.ANY)] * 16,
            out_specs=[whole((8, features + 16, ROWS)), pl.BlockSpec(memory_space=pltpu.HBM)],
            scratch_shapes=[
                pltpu.VMEM((GROUP, WIDTH), BF16),
                pltpu.SemaphoreType.DMA((16,)),
                pltpu.SemaphoreType.DMA,
            ],
        ),
        out_shape=[
            jax.ShapeDtypeStruct((8, features + 16, ROWS), BF16),
            pltpu.HBM((GROUP, WIDTH), BF16),
        ],
        compiler_params=pltpu.CompilerParams(vmem_limit_bytes=20 << 20),
        cost_estimate=pl.CostEstimate(
            flops=2 * GROUP * features * WIDTH, bytes_accessed=10 << 20, transcendentals=0
        ),
        name="head_parts",
    )(place, summaries, rider, *pieces)


def shards(summaries, head, partner):
    core = lax.axis_index("c")
    place = jnp.stack([lax.axis_index(a) for a in ("x", "zl", "y", "zh", "c")]).astype(I32)
    mates = partner.reshape(16, 1, ROWS)

    turned = summaries.T
    mine = lax.dynamic_slice_in_dim(turned, core * HALF, HALF, 1)
    theirs = core_swap(lax.dynamic_slice_in_dim(turned, (1 - core) * HALF, HALF, 1))
    other_head = core_swap(head)
    first_dims = (((0,), (0,)), ((), ()))
    z_part = lax.dot_general(
        mine, head, first_dims, preferred_element_type=F32
    ) + lax.dot_general(theirs, other_head, first_dims, preferred_element_type=F32)
    z_part, place, mates = lax.optimization_barrier((z_part.astype(BF16), place, mates))
    z = sum_exchange(z_part.reshape(8, ROWS, WIDTH), YZ)
    inv = lax.rsqrt(jnp.sum(z * z, axis=1, keepdims=True) + 1e-06)
    unit = z * inv
    emb = unit.astype(BF16)

    keys = gather_ring(emb, "x", "zl")
    queries = gather_ring(emb, "y", "zh")
    queries = queries + [core_swap(piece) for piece in queries]
    weights, row_part, hits, col_part, queries = score_call(place, keys, queries, mates)

    cols = lax.all_to_all(col_part, CUTS, 0, 0)
    row_part = row_part + lax.ppermute(row_part, "zl", SWAP)
    rows = [row_part] + [lax.ppermute(row_part, "x", RING[s]) for s in (1, 3, 2)]
    grad_part, rider = grad_call(place, weights, hits, rows, cols, mates, queries)
    grad_emb = sum_exchange(grad_part.reshape(8, ROWS, WIDTH), XZ)
    grad_z = (inv * (grad_emb - unit * jnp.sum(unit * grad_emb, axis=1, keepdims=True))).astype(BF16)

    pieces = gather_ring(grad_z, "y", "zh")
    pieces = pieces + [core_swap(piece) for piece in pieces]
    head_part, grad_group = head_call(place, turned, rider, pieces)
    pieces = lax.all_to_all(head_part, XZ, 0, 0)
    pieces = jnp.sum(pieces.astype(F32), axis=0)
    features = head.shape[0]
    loss = jnp.sum(pieces[features:, 0]) / TOTAL
    head_sum = pieces[:features].astype(BF16)
    grad_head = spread(head_sum, XZ, 8).transpose(1, 0, 2).reshape(features, WIDTH).astype(F32)

    last_dims = (((1,), (1,)), ((), ()))
    out = lax.dot_general(head, grad_group, last_dims, preferred_element_type=F32).astype(BF16)
    return loss, out.T, grad_head


def solution(mesh):
    fine = Mesh(mesh.devices.reshape(4, 2, 4, 2, 2), ("x", "zl", "y", "zh", "c"))
    return jax.shard_map(
        shards,
        mesh=fine,
        in_specs=(P(XZ, CUTS), P(CUTS, None), P(XZ)),
        out_specs=(P(), P(XZ, CUTS), P(CUTS, None)),
        check_vma=False,
    )
```

```python
import jax
import jax.numpy as jnp
from jax import lax
from jax.experimental import pallas as pl
from jax.experimental.pallas import tpu as pltpu
from jax.sharding import Mesh
from jax.sharding import PartitionSpec as P

F32 = jnp.float32
BF16 = jnp.bfloat16
I32 = jnp.int32
SWAP = [(0, 1), (1, 0)]
RING = {s: [(i, (i + s) % 4) for i in range(4)] for s in (1, 2, 3)}
ROWS = 128
PAIR = 256
HALF = 1024
GROUP = 2048
TOTAL = 16384
WIDTH = 1024
YZ, XZ, CUTS = ("y", "zh"), ("x", "zl"), ("y", "zh", "c")
OFFSET = (0, 1, 3, 2)
EXP2_SCALE = 28.853900817779268


def in_hbm(value):
    return pltpu.with_memory_space_constraint(value, pltpu.HBM)


def core_swap(value):
    return lax.ppermute(value, "c", SWAP)


def spread(value, axes, count):
    return lax.all_to_all(jnp.broadcast_to(value[None], (count,) + value.shape), axes, 0, 0)


def sum_exchange(parts, axes):
    return jnp.sum(lax.all_to_all(parts, axes, 0, 0).astype(F32), axis=0)


def gather_ring(own, long_axis, short_axis, direct=False):
    other = lax.ppermute(own, short_axis, SWAP)
    after_own = lax.ppermute(own, long_axis, RING[3])
    before_own = lax.ppermute(own, long_axis, RING[1])
    far_own = lax.ppermute(after_own, long_axis, RING[3])
    after_other = lax.ppermute(other, long_axis, RING[3])
    before_other = lax.ppermute(other, long_axis, RING[1])
    if direct:
        far_other = lax.ppermute(other, long_axis, RING[2])
    else:
        far_other = lax.ppermute(before_other, long_axis, RING[1])
    return [own, other, after_own, after_other, before_own, before_other, far_own, far_other]


def chunk_of(start, p, which, own_low):
    return lax.rem(start + OFFSET[p], 4) * 2 + (own_low if which == 0 else 1 - own_low)


def key_column(place, p):
    inner = place[4] * HALF + (place[2] * 2 + place[3]) * ROWS
    near, far = (chunk_of(place[0], p, which, place[1]) * GROUP + inner for which in (0, 1))
    at = lax.broadcasted_iota(I32, (PAIR, 1), 0)
    return at % ROWS + jnp.where(at < ROWS, near, far)


def query_core(place, n):
    return place[4] if n < 4 else 1 - place[4]


def query_chunks(place, n):
    return [
        query_core(place, n) * 8 + chunk_of(place[2], n % 4, which, place[3]) for which in (0, 1)
    ]


def score_kernel(place, *refs):
    key_refs, query_refs = refs[:8], refs[8:24]
    (mates, w_ref, row_ref, hit_ref, col_ref, all_ref) = refs[24:30]
    (keys, queries, held, lanes, hit_lanes, sums, key_sem, query_sem, out_sem, all_sem) = refs[30:]
    step = pl.program_id(0)

    def key_copy(i):
        return pltpu.make_async_copy(
            key_refs[i], keys.at[pl.ds(i * ROWS, ROWS), :], key_sem.at[i]
        )

    def query_copies(n):
        return [
            pltpu.make_async_copy(
                query_refs[2 * n + i],
                queries.at[n, pl.ds(i * ROWS, ROWS), :],
                query_sem.at[2 * n + i],
            )
            for i in (0, 1)
        ]

    def all_copy(n):
        return pltpu.make_async_copy(
            queries.at[n], all_ref.at[pl.ds(n * PAIR, PAIR), :], all_sem.at[n]
        )

    def out_copy(n):
        return pltpu.make_async_copy(
            held.at[n % 2], w_ref.at[:, pl.ds(n * PAIR, PAIR)], out_sem.at[n % 2]
        )

    @pl.when(step == 0)
    def _():
        for copy in query_copies(0):
            copy.start()
        for i in range(8):
            key_copy(i).start()
        for n in range(1, 8):
            for copy in query_copies(n):
                copy.start()
        lanes[...] = jnp.zeros_like(lanes)
        hit_lanes[...] = jnp.zeros_like(hit_lanes)
        for i in range(8):
            key_copy(i).wait()

    def run(n, masked):
        for copy in query_copies(n):
            copy.wait()
        all_copy(n).start()
        if n >= 2:
            out_copy(n - 2).wait()
        near, far = query_chunks(place, n)
        mate = jnp.concatenate([mates[near], mates[far]], axis=1)
        col = jnp.zeros((8, PAIR), F32)
        block = lax.dot_general(
            keys[...], queries[n], (((1,), (1,)), ((), ())), preferred_element_type=F32
        )
        for p in range(4):
            at = pl.ds(p * PAIR, PAIR)
            scores = block[p * PAIR : (p + 1) * PAIR]
            kid = key_column(place, p)
            weights = jnp.exp2(scores * EXP2_SCALE)
            if masked and p == 0:
                group = (place[0] * 2 + place[1]) * GROUP
                lane = lax.broadcasted_iota(I32, (1, PAIR), 1)
                qid = group + lane % ROWS + jnp.where(lane < ROWS, near, far) * ROWS
                weights = jnp.where(kid != qid, weights, 0.0)
            held[n % 2, at, :] = weights.astype(BF16)
            lanes[at, :] += weights[:, :ROWS] + weights[:, ROWS:]
            hits = jnp.where(kid == mate, weights, 0.0)
            hit_lanes[at, :] += hits[:, :ROWS] + hits[:, ROWS:]
            col = col + jnp.sum(weights.reshape(PAIR // 8, 8, PAIR), axis=0)
        col = jnp.sum(col, axis=0, keepdims=True)
        sums[pl.ds(near, 1), :] = col[:, :ROWS]
        sums[pl.ds(far, 1), :] = col[:, ROWS:]
        out_copy(n).start()

    for n in range(8):

        @pl.when(step == n)
        def _(n=n):
            run(n, n == 0)

    @pl.when(step == 7)
    def _():
        for p in range(4):
            for which in (0, 1):
                at = pl.ds(p * PAIR + which * ROWS, ROWS)
                chunk = chunk_of(place[0], p, which, place[1])
                hits = jnp.sum(hit_lanes[at, :].T, axis=0, keepdims=True)
                hit_ref[pl.ds(chunk, 1), :] = hits
                row_ref[pl.ds(chunk, 1), :] = jnp.sum(lanes[at, :].T, axis=0, keepdims=True)
                found = hits > 0.0
                sums[16 + 2 * p + which : 17 + 2 * p + which, :] = jnp.where(
                    found, jnp.log(jnp.where(found, hits, 1.0)), 0.0
                )
        for device in range(16):
            col_ref[device] = sums[...]
        out_copy(6).wait()
        out_copy(7).wait()
        for n in range(8):
            all_copy(n).wait()


def grad_kernel(place, w_ref, query_ref, hit_ref, r0, r1, r2, r3, cols_ref, mates, *refs):
    out_ref, rider_ref, weights, queries, w_sem, query_sem, rk_ref, rq_ref = refs

    def w_copy(p):
        return pltpu.make_async_copy(
            w_ref.at[pl.ds(p * PAIR, PAIR), :], weights.at[p], w_sem.at[p]
        )

    query_copy = pltpu.make_async_copy(query_ref, queries, query_sem)

    w_copy(0).start()
    query_copy.start()
    for p in range(1, 4):
        w_copy(p).start()
    cols = cols_ref[0]
    for device in range(1, 16):
        cols = cols + cols_ref[device]
    den = cols[:16]
    rq_ref[...] = 20.0 / den
    rk_ref[...] = 20.0 / (r0[...] + r1[...] + r2[...] + r3[...])
    logs = jnp.sum(jnp.log(den), axis=0, keepdims=True)
    logs = logs - jnp.sum(cols[16:], axis=0, keepdims=True)
    loss = jnp.broadcast_to(jnp.sum(logs, axis=1, keepdims=True), (16, ROWS))
    row = lax.broadcasted_iota(I32, (16, ROWS), 0)
    rider = jnp.zeros((16, ROWS), F32)
    for i in range(3):
        term = loss.astype(BF16).astype(F32)
        rider = jnp.where(row == i, term, rider)
        loss = loss - term
    rider_ref[...] = rider.astype(BF16)

    def columns(source, p):
        chunks = [chunk_of(place[0], p, which, place[1]) for which in (0, 1)]
        return jnp.concatenate(
            [jnp.broadcast_to(source[pl.ds(chunk, 1), :], (ROWS, ROWS)).T for chunk in chunks], axis=0
        )

    def run(p):
        w_copy(p).wait()
        kid = key_column(place, p)
        rk, hit_weights = columns(rk_ref, p), columns(hit_ref, p)
        parts = []
        for n in range(8):
            for which, chunk in enumerate(query_chunks(place, n)):
                start = n * PAIR + which * ROWS
                hit = kid == mates[chunk]
                chosen = jnp.where(hit, hit_weights, weights[p, :, start : start + ROWS].astype(F32))
                grads = chosen * (rk + rq_ref[pl.ds(chunk, 1), :])
                parts.append(jnp.where(hit, grads - 40.0, grads).astype(BF16))
        if p == 0:
            query_copy.wait()
        total = jnp.dot(
            jnp.concatenate(parts, axis=1), queries[...], preferred_element_type=F32
        ).astype(BF16)
        at = lax.rem(place[0] + OFFSET[p], 4)
        out_ref[at, place[1]] = total[:ROWS]
        out_ref[at, 1 - place[1]] = total[ROWS:]

    for p in range(4):
        run(p)


def head_kernel(place, summaries, rider, *refs):
    piece_refs, (head_ref, all_ref, rows, copy_sem, out_sem) = refs[:16], refs[16:]
    features = summaries.shape[0]
    copies = []
    for n in range(8):
        for i, chunk in enumerate(query_chunks(place, n)):
            to = pl.multiple_of(chunk * ROWS, ROWS)
            at = 2 * n + i
            copies.append(
                pltpu.make_async_copy(
                    piece_refs[at], rows.at[pl.ds(to, ROWS), :], copy_sem.at[at]
                )
            )
    for copy in copies:
        copy.start()
    for j in range(8):
        head_ref[j, features:] = rider[...]
    for copy in copies:
        copy.wait()
    out = pltpu.make_async_copy(rows, all_ref, out_sem)
    out.start()
    total = jnp.dot(summaries[...], rows[...], preferred_element_type=F32).astype(BF16)
    for j in range(8):
        head_ref[j, :features] = total[:, j * ROWS : (j + 1) * ROWS]
    out.wait()


def whole(shape):
    return pl.BlockSpec(shape, lambda t, place: (0,) * len(shape))


def score_call(place, keys, queries, mates):
    return pl.pallas_call(
        score_kernel,
        grid_spec=pltpu.PrefetchScalarGridSpec(
            num_scalar_prefetch=1,
            grid=(8,),
            in_specs=[pl.BlockSpec(memory_space=pl.ANY)] * 24 + [whole((16, 1, ROWS))],
            out_specs=[
                pl.BlockSpec(memory_space=pltpu.HBM),
                whole((8, ROWS)),
                whole((8, ROWS)),
                whole((16, 24, ROWS)),
                pl.BlockSpec(memory_space=pltpu.HBM),
            ],
            scratch_shapes=[
                pltpu.VMEM((HALF, WIDTH), BF16),
                pltpu.VMEM((8, PAIR, WIDTH), BF16),
                pltpu.VMEM((2, HALF, PAIR), BF16),
                pltpu.VMEM((HALF, ROWS), F32),
                pltpu.VMEM((HALF, ROWS), F32),
                pltpu.VMEM((24, ROWS), F32),
                pltpu.SemaphoreType.DMA((8,)),
                pltpu.SemaphoreType.DMA((16,)),
                pltpu.SemaphoreType.DMA((2,)),
                pltpu.SemaphoreType.DMA((8,)),
            ],
        ),
        out_shape=[
            pltpu.HBM((HALF, GROUP), BF16),
            jax.ShapeDtypeStruct((8, ROWS), F32),
            jax.ShapeDtypeStruct((8, ROWS), F32),
            jax.ShapeDtypeStruct((16, 24, ROWS), F32),
            pltpu.HBM((GROUP, WIDTH), BF16),
        ],
        compiler_params=pltpu.CompilerParams(vmem_limit_bytes=12 << 20),
        cost_estimate=pl.CostEstimate(
            flops=2 * HALF * GROUP * WIDTH, bytes_accessed=14 << 20, transcendentals=HALF * GROUP
        ),
        name="scores",
    )(place, *keys, *queries, mates)


def grad_call(place, weights, hits, rows, cols, mates, queries):
    return pl.pallas_call(
        grad_kernel,
        grid_spec=pltpu.PrefetchScalarGridSpec(
            num_scalar_prefetch=1,
            grid=(1,),
            in_specs=[pl.BlockSpec(memory_space=pltpu.HBM)] * 2
            + [whole((8, ROWS))] * 5
            + [whole((16, 24, ROWS)), whole((16, 1, ROWS))],
            out_specs=[whole((4, 2, ROWS, WIDTH)), whole((16, ROWS))],
            scratch_shapes=[
                pltpu.VMEM((4, PAIR, GROUP), BF16),
                pltpu.VMEM((GROUP, WIDTH), BF16),
                pltpu.SemaphoreType.DMA((4,)),
                pltpu.SemaphoreType.DMA,
                pltpu.VMEM((8, ROWS), F32),
                pltpu.VMEM((16, ROWS), F32),
            ],
        ),
        out_shape=[
            jax.ShapeDtypeStruct((4, 2, ROWS, WIDTH), BF16),
            jax.ShapeDtypeStruct((16, ROWS), BF16),
        ],
        compiler_params=pltpu.CompilerParams(vmem_limit_bytes=18 << 20),
        cost_estimate=pl.CostEstimate(
            flops=2 * HALF * GROUP * WIDTH, bytes_accessed=14 << 20, transcendentals=0
        ),
        name="grads",
    )(place, in_hbm(weights), in_hbm(queries), hits, *rows, cols, mates)


def head_call(place, summaries, rider, pieces):
    features = summaries.shape[0]
    return pl.pallas_call(
        head_kernel,
        grid_spec=pltpu.PrefetchScalarGridSpec(
            num_scalar_prefetch=1,
            grid=(1,),
            in_specs=[whole((features, GROUP)), whole((16, ROWS))]
            + [pl.BlockSpec(memory_space=pl.ANY)] * 16,
            out_specs=[whole((8, features + 16, ROWS)), pl.BlockSpec(memory_space=pltpu.HBM)],
            scratch_shapes=[
                pltpu.VMEM((GROUP, WIDTH), BF16),
                pltpu.SemaphoreType.DMA((16,)),
                pltpu.SemaphoreType.DMA,
            ],
        ),
        out_shape=[
            jax.ShapeDtypeStruct((8, features + 16, ROWS), BF16),
            pltpu.HBM((GROUP, WIDTH), BF16),
        ],
        compiler_params=pltpu.CompilerParams(vmem_limit_bytes=20 << 20),
        cost_estimate=pl.CostEstimate(
            flops=2 * GROUP * features * WIDTH, bytes_accessed=10 << 20, transcendentals=0
        ),
        name="head_parts",
    )(place, summaries, rider, *pieces)


def shards(summaries, head, partner):
    core = lax.axis_index("c")
    place = jnp.stack([lax.axis_index(a) for a in ("x", "zl", "y", "zh", "c")]).astype(I32)
    mates = partner.reshape(16, 1, ROWS)

    turned = summaries.T
    mine = lax.dynamic_slice_in_dim(turned, core * HALF, HALF, 1)
    theirs = core_swap(lax.dynamic_slice_in_dim(turned, (1 - core) * HALF, HALF, 1))
    other_head = core_swap(head)
    first_dims = (((0,), (0,)), ((), ()))
    z_part = lax.dot_general(
        mine, head, first_dims, preferred_element_type=F32
    ) + lax.dot_general(theirs, other_head, first_dims, preferred_element_type=F32)
    z_part, place, mates = lax.optimization_barrier((z_part.astype(BF16), place, mates))
    z = sum_exchange(z_part.reshape(8, ROWS, WIDTH), YZ)
    inv = lax.rsqrt(jnp.sum(z * z, axis=1, keepdims=True) + 1e-06)
    unit = z * inv
    emb = unit.astype(BF16)

    keys = gather_ring(emb, "x", "zl", direct=True)
    queries = gather_ring(emb, "y", "zh")
    queries = queries + [core_swap(piece) for piece in queries]
    weights, row_part, hits, col_part, queries = score_call(place, keys, queries, mates)

    cols = lax.all_to_all(col_part, CUTS, 0, 0)
    row_part = row_part + lax.ppermute(row_part, "zl", SWAP)
    rows = [row_part] + [lax.ppermute(row_part, "x", RING[s]) for s in (1, 3, 2)]
    grad_part, rider = grad_call(place, weights, hits, rows, cols, mates, queries)
    grad_emb = sum_exchange(grad_part.reshape(8, ROWS, WIDTH), XZ)
    grad_z = (inv * (grad_emb - unit * jnp.sum(unit * grad_emb, axis=1, keepdims=True))).astype(BF16)

    pieces = gather_ring(grad_z, "y", "zh")
    pieces = pieces + [core_swap(piece) for piece in pieces]
    head_part, grad_group = head_call(place, turned, rider, pieces)
    pieces = lax.all_to_all(head_part, XZ, 0, 0)
    pieces = jnp.sum(pieces.astype(F32), axis=0)
    features = head.shape[0]
    loss = jnp.sum(pieces[features:, 0]) / TOTAL
    head_sum = pieces[:features].astype(BF16)
    grad_head = spread(head_sum, XZ, 8).transpose(1, 0, 2).reshape(features, WIDTH).astype(F32)

    last_dims = (((1,), (1,)), ((), ()))
    out = lax.dot_general(head, grad_group, last_dims, preferred_element_type=F32).astype(BF16)
    return loss, out.T, grad_head


def solution(mesh):
    fine = Mesh(mesh.devices.reshape(4, 2, 4, 2, 2), ("x", "zl", "y", "zh", "c"))
    return jax.shard_map(
        shards,
        mesh=fine,
        in_specs=(P(XZ, CUTS), P(CUTS, None), P(XZ)),
        out_specs=(P(), P(XZ, CUTS), P(CUTS, None)),
        check_vma=False,
    )
```

```python
import jax
import jax.numpy as jnp
from jax import lax
from jax.experimental import pallas as pl
from jax.experimental.pallas import tpu as pltpu
from jax.sharding import Mesh
from jax.sharding import PartitionSpec as P

F32 = jnp.float32
BF16 = jnp.bfloat16
I32 = jnp.int32
SWAP = [(0, 1), (1, 0)]
RING = {s: [(i, (i + s) % 4) for i in range(4)] for s in (1, 2, 3)}
ROWS = 128
PAIR = 256
HALF = 1024
GROUP = 2048
TOTAL = 16384
WIDTH = 1024
YZ, XZ, CUTS = ("y", "zh"), ("x", "zl"), ("y", "zh", "c")
OFFSET = (0, 1, 3, 2)
EXP2_SCALE = 28.853900817779268


def in_hbm(value):
    return pltpu.with_memory_space_constraint(value, pltpu.HBM)


def core_swap(value):
    return lax.ppermute(value, "c", SWAP)


def spread(value, axes, count):
    return lax.all_to_all(jnp.broadcast_to(value[None], (count,) + value.shape), axes, 0, 0)


def sum_exchange(parts, axes):
    return jnp.sum(lax.all_to_all(parts, axes, 0, 0).astype(F32), axis=0)


def gather_ring(own, long_axis, short_axis, direct=False):
    other = lax.ppermute(own, short_axis, SWAP)
    after_own = lax.ppermute(own, long_axis, RING[3])
    before_own = lax.ppermute(own, long_axis, RING[1])
    far_own = lax.ppermute(after_own, long_axis, RING[3])
    after_other = lax.ppermute(other, long_axis, RING[3])
    before_other = lax.ppermute(other, long_axis, RING[1])
    if direct:
        far_other = lax.ppermute(other, long_axis, RING[2])
    else:
        far_other = lax.ppermute(before_other, long_axis, RING[1])
    return [own, other, after_own, after_other, before_own, before_other, far_own, far_other]


def chunk_of(start, p, which, own_low):
    return lax.rem(start + OFFSET[p], 4) * 2 + (own_low if which == 0 else 1 - own_low)


def key_column(place, p):
    inner = place[4] * HALF + (place[2] * 2 + place[3]) * ROWS
    near, far = (chunk_of(place[0], p, which, place[1]) * GROUP + inner for which in (0, 1))
    at = lax.broadcasted_iota(I32, (PAIR, 1), 0)
    return at % ROWS + jnp.where(at < ROWS, near, far)


def query_core(place, n):
    return place[4] if n < 4 else 1 - place[4]


def query_chunks(place, n):
    return [
        query_core(place, n) * 8 + chunk_of(place[2], n % 4, which, place[3]) for which in (0, 1)
    ]


def score_kernel(place, *refs):
    key_refs, query_refs = refs[:8], refs[8:24]
    (mates, w_ref, row_ref, hit_ref, col_ref, all_ref) = refs[24:30]
    (keys, queries, held, lanes, hit_lanes, sums, key_sem, query_sem, out_sem, all_sem) = refs[30:]
    step = pl.program_id(0)

    def key_copy(i):
        return pltpu.make_async_copy(
            key_refs[i], keys.at[pl.ds(i * ROWS, ROWS), :], key_sem.at[i]
        )

    def query_copies(n):
        return [
            pltpu.make_async_copy(
                query_refs[2 * n + i],
                queries.at[n, pl.ds(i * ROWS, ROWS), :],
                query_sem.at[2 * n + i],
            )
            for i in (0, 1)
        ]

    def all_copy(n):
        return pltpu.make_async_copy(
            queries.at[n], all_ref.at[pl.ds(n * PAIR, PAIR), :], all_sem.at[n]
        )

    def out_copy(n):
        return pltpu.make_async_copy(
            held.at[n % 2], w_ref.at[:, pl.ds(n * PAIR, PAIR)], out_sem.at[n % 2]
        )

    @pl.when(step == 0)
    def _():
        for copy in query_copies(0):
            copy.start()
        for i in range(8):
            key_copy(i).start()
        for n in range(1, 8):
            for copy in query_copies(n):
                copy.start()
        lanes[...] = jnp.zeros_like(lanes)
        hit_lanes[...] = jnp.zeros_like(hit_lanes)
        for i in range(8):
            key_copy(i).wait()

    def run(n, masked):
        for copy in query_copies(n):
            copy.wait()
        all_copy(n).start()
        if n >= 2:
            out_copy(n - 2).wait()
        near, far = query_chunks(place, n)
        mate = jnp.concatenate([mates[near], mates[far]], axis=1)
        col = jnp.zeros((8, PAIR), F32)
        block = lax.dot_general(
            keys[...], queries[n], (((1,), (1,)), ((), ())), preferred_element_type=F32
        )
        for p in range(4):
            at = pl.ds(p * PAIR, PAIR)
            scores = block[p * PAIR : (p + 1) * PAIR]
            kid = key_column(place, p)
            weights = jnp.exp2(scores * EXP2_SCALE)
            if masked and p == 0:
                group = (place[0] * 2 + place[1]) * GROUP
                lane = lax.broadcasted_iota(I32, (1, PAIR), 1)
                qid = group + lane % ROWS + jnp.where(lane < ROWS, near, far) * ROWS
                weights = jnp.where(kid != qid, weights, 0.0)
            held[n % 2, at, :] = weights.astype(BF16)
            lanes[at, :] += weights[:, :ROWS] + weights[:, ROWS:]
            hits = jnp.where(kid == mate, weights, 0.0)
            hit_lanes[at, :] += hits[:, :ROWS] + hits[:, ROWS:]
            col = col + jnp.sum(weights.reshape(PAIR // 8, 8, PAIR), axis=0)
        col = jnp.sum(col, axis=0, keepdims=True)
        sums[pl.ds(near, 1), :] = col[:, :ROWS]
        sums[pl.ds(far, 1), :] = col[:, ROWS:]
        out_copy(n).start()

    for n in range(8):

        @pl.when(step == n)
        def _(n=n):
            run(n, n == 0)

    @pl.when(step == 7)
    def _():
        for p in range(4):
            for which in (0, 1):
                at = pl.ds(p * PAIR + which * ROWS, ROWS)
                chunk = chunk_of(place[0], p, which, place[1])
                hits = jnp.sum(hit_lanes[at, :].T, axis=0, keepdims=True)
                hit_ref[pl.ds(chunk, 1), :] = hits
                row_ref[pl.ds(chunk, 1), :] = jnp.sum(lanes[at, :].T, axis=0, keepdims=True)
                found = hits > 0.0
                sums[16 + 2 * p + which : 17 + 2 * p + which, :] = jnp.where(
                    found, jnp.log(jnp.where(found, hits, 1.0)), 0.0
                )
        for device in range(16):
            col_ref[device] = sums[...]
        out_copy(6).wait()
        out_copy(7).wait()
        for n in range(8):
            all_copy(n).wait()


def grad_kernel(place, w_ref, query_ref, hit_ref, r0, r1, r2, r3, cols_ref, mates, *refs):
    out_ref, rider_ref, weights, queries, w_sem, query_sem, rk_ref, rq_ref = refs

    def w_copy(p):
        return pltpu.make_async_copy(
            w_ref.at[pl.ds(p * PAIR, PAIR), :], weights.at[p], w_sem.at[p]
        )

    query_copy = pltpu.make_async_copy(query_ref, queries, query_sem)

    w_copy(0).start()
    query_copy.start()
    for p in range(1, 4):
        w_copy(p).start()
    cols = cols_ref[0]
    for device in range(1, 16):
        cols = cols + cols_ref[device]
    den = cols[:16]
    rq_ref[...] = 20.0 / den
    rk_ref[...] = 20.0 / (r0[...] + r1[...] + r2[...] + r3[...])
    logs = jnp.sum(jnp.log(den), axis=0, keepdims=True)
    logs = logs - jnp.sum(cols[16:], axis=0, keepdims=True)
    loss = jnp.broadcast_to(jnp.sum(logs, axis=1, keepdims=True), (16, ROWS))
    row = lax.broadcasted_iota(I32, (16, ROWS), 0)
    rider = jnp.zeros((16, ROWS), F32)
    for i in range(3):
        term = loss.astype(BF16).astype(F32)
        rider = jnp.where(row == i, term, rider)
        loss = loss - term
    rider_ref[...] = rider.astype(BF16)

    def columns(source, p):
        chunks = [chunk_of(place[0], p, which, place[1]) for which in (0, 1)]
        return jnp.concatenate(
            [jnp.broadcast_to(source[pl.ds(chunk, 1), :], (ROWS, ROWS)).T for chunk in chunks], axis=0
        )

    def run(p):
        w_copy(p).wait()
        kid = key_column(place, p)
        rk, hit_weights = columns(rk_ref, p), columns(hit_ref, p)
        parts = []
        for n in range(8):
            for which, chunk in enumerate(query_chunks(place, n)):
                start = n * PAIR + which * ROWS
                hit = kid == mates[chunk]
                chosen = jnp.where(hit, hit_weights, weights[p, :, start : start + ROWS].astype(F32))
                grads = chosen * (rk + rq_ref[pl.ds(chunk, 1), :])
                parts.append(jnp.where(hit, grads - 40.0, grads).astype(BF16))
        if p == 0:
            query_copy.wait()
        total = jnp.dot(
            jnp.concatenate(parts, axis=1), queries[...], preferred_element_type=F32
        ).astype(BF16)
        at = lax.rem(place[0] + OFFSET[p], 4)
        out_ref[at, place[1]] = total[:ROWS]
        out_ref[at, 1 - place[1]] = total[ROWS:]

    for p in range(4):
        run(p)


def head_kernel(place, summaries, rider, *refs):
    piece_refs, (head_ref, all_ref, rows, copy_sem, out_sem) = refs[:16], refs[16:]
    features = summaries.shape[0]
    copies, outs = [], []
    for n in range(8):
        for i, chunk in enumerate(query_chunks(place, n)):
            to = pl.ds(pl.multiple_of(chunk * ROWS, ROWS), ROWS)
            at = 2 * n + i
            copies.append(
                pltpu.make_async_copy(piece_refs[at], rows.at[to, :], copy_sem.at[at])
            )
            outs.append(pltpu.make_async_copy(piece_refs[at], all_ref.at[to, :], out_sem.at[at]))
    for copy in copies + outs:
        copy.start()
    for j in range(8):
        head_ref[j, features:] = rider[...]
    for copy in copies:
        copy.wait()
    total = jnp.dot(summaries[...], rows[...], preferred_element_type=F32).astype(BF16)
    for j in range(8):
        head_ref[j, :features] = total[:, j * ROWS : (j + 1) * ROWS]
    for out in outs:
        out.wait()


def whole(shape):
    return pl.BlockSpec(shape, lambda t, place: (0,) * len(shape))


def score_call(place, keys, queries, mates):
    return pl.pallas_call(
        score_kernel,
        grid_spec=pltpu.PrefetchScalarGridSpec(
            num_scalar_prefetch=1,
            grid=(8,),
            in_specs=[pl.BlockSpec(memory_space=pl.ANY)] * 24 + [whole((16, 1, ROWS))],
            out_specs=[
                pl.BlockSpec(memory_space=pltpu.HBM),
                whole((8, ROWS)),
                whole((8, ROWS)),
                whole((16, 24, ROWS)),
                pl.BlockSpec(memory_space=pltpu.HBM),
            ],
            scratch_shapes=[
                pltpu.VMEM((HALF, WIDTH), BF16),
                pltpu.VMEM((8, PAIR, WIDTH), BF16),
                pltpu.VMEM((2, HALF, PAIR), BF16),
                pltpu.VMEM((HALF, ROWS), F32),
                pltpu.VMEM((HALF, ROWS), F32),
                pltpu.VMEM((24, ROWS), F32),
                pltpu.SemaphoreType.DMA((8,)),
                pltpu.SemaphoreType.DMA((16,)),
                pltpu.SemaphoreType.DMA((2,)),
                pltpu.SemaphoreType.DMA((8,)),
            ],
        ),
        out_shape=[
            pltpu.HBM((HALF, GROUP), BF16),
            jax.ShapeDtypeStruct((8, ROWS), F32),
            jax.ShapeDtypeStruct((8, ROWS), F32),
            jax.ShapeDtypeStruct((16, 24, ROWS), F32),
            pltpu.HBM((GROUP, WIDTH), BF16),
        ],
        compiler_params=pltpu.CompilerParams(vmem_limit_bytes=12 << 20),
        cost_estimate=pl.CostEstimate(
            flops=2 * HALF * GROUP * WIDTH, bytes_accessed=14 << 20, transcendentals=HALF * GROUP
        ),
        name="scores",
    )(place, *keys, *queries, mates)


def grad_call(place, weights, hits, rows, cols, mates, queries):
    return pl.pallas_call(
        grad_kernel,
        grid_spec=pltpu.PrefetchScalarGridSpec(
            num_scalar_prefetch=1,
            grid=(1,),
            in_specs=[pl.BlockSpec(memory_space=pltpu.HBM)] * 2
            + [whole((8, ROWS))] * 5
            + [whole((16, 24, ROWS)), whole((16, 1, ROWS))],
            out_specs=[whole((4, 2, ROWS, WIDTH)), whole((16, ROWS))],
            scratch_shapes=[
                pltpu.VMEM((4, PAIR, GROUP), BF16),
                pltpu.VMEM((GROUP, WIDTH), BF16),
                pltpu.SemaphoreType.DMA((4,)),
                pltpu.SemaphoreType.DMA,
                pltpu.VMEM((8, ROWS), F32),
                pltpu.VMEM((16, ROWS), F32),
            ],
        ),
        out_shape=[
            jax.ShapeDtypeStruct((4, 2, ROWS, WIDTH), BF16),
            jax.ShapeDtypeStruct((16, ROWS), BF16),
        ],
        compiler_params=pltpu.CompilerParams(vmem_limit_bytes=18 << 20),
        cost_estimate=pl.CostEstimate(
            flops=2 * HALF * GROUP * WIDTH, bytes_accessed=14 << 20, transcendentals=0
        ),
        name="grads",
    )(place, in_hbm(weights), in_hbm(queries), hits, *rows, cols, mates)


def head_call(place, summaries, rider, pieces):
    features = summaries.shape[0]
    return pl.pallas_call(
        head_kernel,
        grid_spec=pltpu.PrefetchScalarGridSpec(
            num_scalar_prefetch=1,
            grid=(1,),
            in_specs=[whole((features, GROUP)), whole((16, ROWS))]
            + [pl.BlockSpec(memory_space=pl.ANY)] * 16,
            out_specs=[whole((8, features + 16, ROWS)), pl.BlockSpec(memory_space=pltpu.HBM)],
            scratch_shapes=[
                pltpu.VMEM((GROUP, WIDTH), BF16),
                pltpu.SemaphoreType.DMA((16,)),
                pltpu.SemaphoreType.DMA((16,)),
            ],
        ),
        out_shape=[
            jax.ShapeDtypeStruct((8, features + 16, ROWS), BF16),
            pltpu.HBM((GROUP, WIDTH), BF16),
        ],
        compiler_params=pltpu.CompilerParams(vmem_limit_bytes=20 << 20),
        cost_estimate=pl.CostEstimate(
            flops=2 * GROUP * features * WIDTH, bytes_accessed=10 << 20, transcendentals=0
        ),
        name="head_parts",
    )(place, summaries, rider, *pieces)


def shards(summaries, head, partner):
    core = lax.axis_index("c")
    place = jnp.stack([lax.axis_index(a) for a in ("x", "zl", "y", "zh", "c")]).astype(I32)
    mates = partner.reshape(16, 1, ROWS)

    turned = summaries.T
    mine = lax.dynamic_slice_in_dim(turned, core * HALF, HALF, 1)
    theirs = core_swap(lax.dynamic_slice_in_dim(turned, (1 - core) * HALF, HALF, 1))
    other_head = core_swap(head)
    first_dims = (((0,), (0,)), ((), ()))
    z_part = lax.dot_general(
        mine, head, first_dims, preferred_element_type=F32
    ) + lax.dot_general(theirs, other_head, first_dims, preferred_element_type=F32)
    z_part, place, mates = lax.optimization_barrier((z_part.astype(BF16), place, mates))
    z = sum_exchange(z_part.reshape(8, ROWS, WIDTH), YZ)
    inv = lax.rsqrt(jnp.sum(z * z, axis=1, keepdims=True) + 1e-06)
    unit = z * inv
    emb = unit.astype(BF16)

    keys = gather_ring(emb, "x", "zl", direct=True)
    queries = gather_ring(emb, "y", "zh")
    queries = queries + [core_swap(piece) for piece in queries]
    weights, row_part, hits, col_part, queries = score_call(place, keys, queries, mates)

    cols = lax.all_to_all(col_part, CUTS, 0, 0)
    row_part = row_part + lax.ppermute(row_part, "zl", SWAP)
    rows = [row_part] + [lax.ppermute(row_part, "x", RING[s]) for s in (1, 3, 2)]
    grad_part, rider = grad_call(place, weights, hits, rows, cols, mates, queries)
    grad_emb = sum_exchange(grad_part.reshape(8, ROWS, WIDTH), XZ)
    grad_z = (inv * (grad_emb - unit * jnp.sum(unit * grad_emb, axis=1, keepdims=True))).astype(BF16)

    pieces = gather_ring(grad_z, "y", "zh")
    pieces = pieces + [core_swap(piece) for piece in pieces]
    head_part, grad_group = head_call(place, turned, rider, pieces)
    pieces = lax.all_to_all(head_part, XZ, 0, 0)
    pieces = jnp.sum(pieces.astype(F32), axis=0)
    features = head.shape[0]
    loss = jnp.sum(pieces[features:, 0]) / TOTAL
    head_sum = pieces[:features].astype(BF16)
    grad_head = spread(head_sum, XZ, 8).transpose(1, 0, 2).reshape(features, WIDTH).astype(F32)

    last_dims = (((1,), (1,)), ((), ()))
    out = lax.dot_general(head, grad_group, last_dims, preferred_element_type=F32).astype(BF16)
    return loss, out.T, grad_head


def solution(mesh):
    fine = Mesh(mesh.devices.reshape(4, 2, 4, 2, 2), ("x", "zl", "y", "zh", "c"))
    return jax.shard_map(
        shards,
        mesh=fine,
        in_specs=(P(XZ, CUTS), P(CUTS, None), P(XZ)),
        out_specs=(P(), P(XZ, CUTS), P(CUTS, None)),
        check_vma=False,
    )
```

```python
import jax
import jax.numpy as jnp
from jax import lax
from jax.experimental import pallas as pl
from jax.experimental.pallas import tpu as pltpu
from jax.sharding import Mesh
from jax.sharding import PartitionSpec as P

F32 = jnp.float32
BF16 = jnp.bfloat16
I32 = jnp.int32
SWAP = [(0, 1), (1, 0)]
RING = {s: [(i, (i + s) % 4) for i in range(4)] for s in (1, 2, 3)}
ROWS = 128
PAIR = 256
HALF = 1024
GROUP = 2048
TOTAL = 16384
WIDTH = 1024
YZ, XZ, CUTS = ("y", "zh"), ("x", "zl"), ("y", "zh", "c")
OFFSET = (0, 1, 3, 2)
EXP2_SCALE = 28.853900817779268


def in_hbm(value):
    return pltpu.with_memory_space_constraint(value, pltpu.HBM)


def core_swap(value):
    return lax.ppermute(value, "c", SWAP)


def spread(value, axes, count):
    return lax.all_to_all(jnp.broadcast_to(value[None], (count,) + value.shape), axes, 0, 0)


def sum_exchange(parts, axes):
    return jnp.sum(lax.all_to_all(parts, axes, 0, 0).astype(F32), axis=0)


def gather_ring(own, long_axis, short_axis, direct=False):
    other = lax.ppermute(own, short_axis, SWAP)
    after_own = lax.ppermute(own, long_axis, RING[3])
    before_own = lax.ppermute(own, long_axis, RING[1])
    far_own = lax.ppermute(after_own, long_axis, RING[3])
    after_other = lax.ppermute(other, long_axis, RING[3])
    before_other = lax.ppermute(other, long_axis, RING[1])
    if direct:
        far_other = lax.ppermute(other, long_axis, RING[2])
    else:
        far_other = lax.ppermute(before_other, long_axis, RING[1])
    return [own, other, after_own, after_other, before_own, before_other, far_own, far_other]


def chunk_of(start, p, which, own_low):
    return lax.rem(start + OFFSET[p], 4) * 2 + (own_low if which == 0 else 1 - own_low)


def key_column(place, p):
    inner = place[4] * HALF + (place[2] * 2 + place[3]) * ROWS
    near, far = (chunk_of(place[0], p, which, place[1]) * GROUP + inner for which in (0, 1))
    at = lax.broadcasted_iota(I32, (PAIR, 1), 0)
    return at % ROWS + jnp.where(at < ROWS, near, far)


def query_core(place, n):
    return place[4] if n < 4 else 1 - place[4]


def query_chunks(place, n):
    return [
        query_core(place, n) * 8 + chunk_of(place[2], n % 4, which, place[3]) for which in (0, 1)
    ]


def score_kernel(place, *refs):
    key_refs, query_refs = refs[:8], refs[8:24]
    (mates, w_ref, row_ref, hit_ref, col_ref, all_ref) = refs[24:30]
    (keys, queries, held, lanes, hit_lanes, sums, key_sem, query_sem, out_sem, all_sem) = refs[30:]
    step = pl.program_id(0)

    def key_copy(i):
        return pltpu.make_async_copy(
            key_refs[i], keys.at[pl.ds(i * ROWS, ROWS), :], key_sem.at[i]
        )

    def query_copies(n):
        return [
            pltpu.make_async_copy(
                query_refs[2 * n + i],
                queries.at[n, pl.ds(i * ROWS, ROWS), :],
                query_sem.at[2 * n + i],
            )
            for i in (0, 1)
        ]

    def all_copy(n):
        return pltpu.make_async_copy(
            queries.at[n], all_ref.at[pl.ds(n * PAIR, PAIR), :], all_sem.at[n]
        )

    def out_copy(n):
        return pltpu.make_async_copy(
            held.at[n % 2], w_ref.at[:, pl.ds(n * PAIR, PAIR)], out_sem.at[n % 2]
        )

    @pl.when(step == 0)
    def _():
        for copy in query_copies(0):
            copy.start()
        for i in range(8):
            key_copy(i).start()
        for n in range(1, 8):
            for copy in query_copies(n):
                copy.start()
        lanes[...] = jnp.zeros_like(lanes)
        hit_lanes[...] = jnp.zeros_like(hit_lanes)
        for i in range(8):
            key_copy(i).wait()

    def run(n, masked):
        for copy in query_copies(n):
            copy.wait()
        all_copy(n).start()
        if n >= 2:
            out_copy(n - 2).wait()
        near, far = query_chunks(place, n)
        mate = jnp.concatenate([mates[near], mates[far]], axis=1)
        col = jnp.zeros((8, PAIR), F32)
        block = lax.dot_general(
            keys[...], queries[n], (((1,), (1,)), ((), ())), preferred_element_type=F32
        )
        for p in range(4):
            at = pl.ds(p * PAIR, PAIR)
            scores = block[p * PAIR : (p + 1) * PAIR]
            kid = key_column(place, p)
            weights = jnp.exp2(scores * EXP2_SCALE)
            if masked and p == 0:
                group = (place[0] * 2 + place[1]) * GROUP
                lane = lax.broadcasted_iota(I32, (1, PAIR), 1)
                qid = group + lane % ROWS + jnp.where(lane < ROWS, near, far) * ROWS
                weights = jnp.where(kid != qid, weights, 0.0)
            held[n % 2, at, :] = weights.astype(BF16)
            lanes[at, :] += weights[:, :ROWS] + weights[:, ROWS:]
            hits = jnp.where(kid == mate, weights, 0.0)
            hit_lanes[at, :] += hits[:, :ROWS] + hits[:, ROWS:]
            col = col + jnp.sum(weights.reshape(PAIR // 8, 8, PAIR), axis=0)
        col = jnp.sum(col, axis=0, keepdims=True)
        sums[pl.ds(near, 1), :] = col[:, :ROWS]
        sums[pl.ds(far, 1), :] = col[:, ROWS:]
        out_copy(n).start()

    for n in range(8):

        @pl.when(step == n)
        def _(n=n):
            run(n, n == 0)

    @pl.when(step == 7)
    def _():
        for p in range(4):
            for which in (0, 1):
                at = pl.ds(p * PAIR + which * ROWS, ROWS)
                chunk = chunk_of(place[0], p, which, place[1])
                hits = jnp.sum(hit_lanes[at, :].T, axis=0, keepdims=True)
                hit_ref[pl.ds(chunk, 1), :] = hits
                row_ref[pl.ds(chunk, 1), :] = jnp.sum(lanes[at, :].T, axis=0, keepdims=True)
                found = hits > 0.0
                sums[16 + 2 * p + which : 17 + 2 * p + which, :] = jnp.where(
                    found, jnp.log(jnp.where(found, hits, 1.0)), 0.0
                )
        for device in range(16):
            col_ref[device] = sums[...]
        out_copy(6).wait()
        out_copy(7).wait()
        for n in range(8):
            all_copy(n).wait()


def grad_kernel(place, w_ref, query_ref, hit_ref, r0, r1, r2, r3, cols_ref, mates, *refs):
    out_ref, rider_ref, weights, queries, w_sem, query_sem, rk_ref, rq_ref = refs

    def w_copy(p):
        return pltpu.make_async_copy(
            w_ref.at[pl.ds(p * PAIR, PAIR), :], weights.at[p], w_sem.at[p]
        )

    query_copy = pltpu.make_async_copy(query_ref, queries, query_sem)

    w_copy(0).start()
    query_copy.start()
    for p in range(1, 4):
        w_copy(p).start()
    cols = cols_ref[0]
    for device in range(1, 16):
        cols = cols + cols_ref[device]
    den = cols[:16]
    rq_ref[...] = 20.0 / den
    rk_ref[...] = 20.0 / (r0[...] + r1[...] + r2[...] + r3[...])
    logs = jnp.sum(jnp.log(den), axis=0, keepdims=True)
    logs = logs - jnp.sum(cols[16:], axis=0, keepdims=True)
    loss = jnp.broadcast_to(jnp.sum(logs, axis=1, keepdims=True), (16, ROWS))
    row = lax.broadcasted_iota(I32, (16, ROWS), 0)
    rider = jnp.zeros((16, ROWS), F32)
    for i in range(3):
        term = loss.astype(BF16).astype(F32)
        rider = jnp.where(row == i, term, rider)
        loss = loss - term
    rider_ref[...] = rider.astype(BF16)

    def columns(source, p):
        chunks = [chunk_of(place[0], p, which, place[1]) for which in (0, 1)]
        return jnp.concatenate(
            [jnp.broadcast_to(source[pl.ds(chunk, 1), :], (ROWS, ROWS)).T for chunk in chunks], axis=0
        )

    def run(p):
        w_copy(p).wait()
        kid = key_column(place, p)
        rk, hit_weights = columns(rk_ref, p), columns(hit_ref, p)
        parts = []
        for n in range(8):
            for which, chunk in enumerate(query_chunks(place, n)):
                start = n * PAIR + which * ROWS
                hit = kid == mates[chunk]
                chosen = jnp.where(hit, hit_weights, weights[p, :, start : start + ROWS].astype(F32))
                grads = chosen * (rk + rq_ref[pl.ds(chunk, 1), :])
                parts.append(jnp.where(hit, grads - 40.0, grads).astype(BF16))
        if p == 0:
            query_copy.wait()
        total = jnp.dot(
            jnp.concatenate(parts, axis=1), queries[...], preferred_element_type=F32
        ).astype(BF16)
        at = lax.rem(place[0] + OFFSET[p], 4)
        out_ref[at, place[1]] = total[:ROWS]
        out_ref[at, 1 - place[1]] = total[ROWS:]

    for p in range(4):
        run(p)


def head_kernel(place, summaries, rider, *refs):
    piece_refs, (head_ref, all_ref, rows, held, held_sem, copy_sem, out_sem) = refs[:16], refs[16:]
    features = summaries.shape[0]
    copies, outs = [pltpu.make_async_copy(summaries, held, held_sem)], []
    for n in range(8):
        for i, chunk in enumerate(query_chunks(place, n)):
            to = pl.ds(pl.multiple_of(chunk * ROWS, ROWS), ROWS)
            at = 2 * n + i
            copies.append(
                pltpu.make_async_copy(piece_refs[at], rows.at[to, :], copy_sem.at[at])
            )
            outs.append(pltpu.make_async_copy(piece_refs[at], all_ref.at[to, :], out_sem.at[at]))
    for copy in copies + outs:
        copy.start()
    for j in range(8):
        head_ref[j, features:] = rider[...]
    for copy in copies:
        copy.wait()
    total = jnp.dot(held[...], rows[...], preferred_element_type=F32).astype(BF16)
    for j in range(8):
        head_ref[j, :features] = total[:, j * ROWS : (j + 1) * ROWS]
    for out in outs:
        out.wait()


def whole(shape):
    return pl.BlockSpec(shape, lambda t, place: (0,) * len(shape))


def score_call(place, keys, queries, mates):
    return pl.pallas_call(
        score_kernel,
        grid_spec=pltpu.PrefetchScalarGridSpec(
            num_scalar_prefetch=1,
            grid=(8,),
            in_specs=[pl.BlockSpec(memory_space=pl.ANY)] * 24 + [whole((16, 1, ROWS))],
            out_specs=[
                pl.BlockSpec(memory_space=pltpu.HBM),
                whole((8, ROWS)),
                whole((8, ROWS)),
                whole((16, 24, ROWS)),
                pl.BlockSpec(memory_space=pltpu.HBM),
            ],
            scratch_shapes=[
                pltpu.VMEM((HALF, WIDTH), BF16),
                pltpu.VMEM((8, PAIR, WIDTH), BF16),
                pltpu.VMEM((2, HALF, PAIR), BF16),
                pltpu.VMEM((HALF, ROWS), F32),
                pltpu.VMEM((HALF, ROWS), F32),
                pltpu.VMEM((24, ROWS), F32),
                pltpu.SemaphoreType.DMA((8,)),
                pltpu.SemaphoreType.DMA((16,)),
                pltpu.SemaphoreType.DMA((2,)),
                pltpu.SemaphoreType.DMA((8,)),
            ],
        ),
        out_shape=[
            pltpu.HBM((HALF, GROUP), BF16),
            jax.ShapeDtypeStruct((8, ROWS), F32),
            jax.ShapeDtypeStruct((8, ROWS), F32),
            jax.ShapeDtypeStruct((16, 24, ROWS), F32),
            pltpu.HBM((GROUP, WIDTH), BF16),
        ],
        compiler_params=pltpu.CompilerParams(vmem_limit_bytes=12 << 20),
        cost_estimate=pl.CostEstimate(
            flops=2 * HALF * GROUP * WIDTH, bytes_accessed=14 << 20, transcendentals=HALF * GROUP
        ),
        name="scores",
    )(place, *keys, *queries, mates)


def grad_call(place, weights, hits, rows, cols, mates, queries):
    return pl.pallas_call(
        grad_kernel,
        grid_spec=pltpu.PrefetchScalarGridSpec(
            num_scalar_prefetch=1,
            grid=(1,),
            in_specs=[pl.BlockSpec(memory_space=pltpu.HBM)] * 2
            + [whole((8, ROWS))] * 5
            + [whole((16, 24, ROWS)), whole((16, 1, ROWS))],
            out_specs=[whole((4, 2, ROWS, WIDTH)), whole((16, ROWS))],
            scratch_shapes=[
                pltpu.VMEM((4, PAIR, GROUP), BF16),
                pltpu.VMEM((GROUP, WIDTH), BF16),
                pltpu.SemaphoreType.DMA((4,)),
                pltpu.SemaphoreType.DMA,
                pltpu.VMEM((8, ROWS), F32),
                pltpu.VMEM((16, ROWS), F32),
            ],
        ),
        out_shape=[
            jax.ShapeDtypeStruct((4, 2, ROWS, WIDTH), BF16),
            jax.ShapeDtypeStruct((16, ROWS), BF16),
        ],
        compiler_params=pltpu.CompilerParams(vmem_limit_bytes=18 << 20),
        cost_estimate=pl.CostEstimate(
            flops=2 * HALF * GROUP * WIDTH, bytes_accessed=14 << 20, transcendentals=0
        ),
        name="grads",
    )(place, in_hbm(weights), in_hbm(queries), hits, *rows, cols, mates)


def head_call(place, summaries, rider, pieces):
    features = summaries.shape[0]
    return pl.pallas_call(
        head_kernel,
        grid_spec=pltpu.PrefetchScalarGridSpec(
            num_scalar_prefetch=1,
            grid=(1,),
            in_specs=[pl.BlockSpec(memory_space=pl.ANY), whole((16, ROWS))]
            + [pl.BlockSpec(memory_space=pl.ANY)] * 16,
            out_specs=[whole((8, features + 16, ROWS)), pl.BlockSpec(memory_space=pltpu.HBM)],
            scratch_shapes=[
                pltpu.VMEM((GROUP, WIDTH), BF16),
                pltpu.VMEM((features, GROUP), BF16),
                pltpu.SemaphoreType.DMA,
                pltpu.SemaphoreType.DMA((16,)),
                pltpu.SemaphoreType.DMA((16,)),
            ],
        ),
        out_shape=[
            jax.ShapeDtypeStruct((8, features + 16, ROWS), BF16),
            pltpu.HBM((GROUP, WIDTH), BF16),
        ],
        compiler_params=pltpu.CompilerParams(vmem_limit_bytes=20 << 20),
        cost_estimate=pl.CostEstimate(
            flops=2 * GROUP * features * WIDTH, bytes_accessed=10 << 20, transcendentals=0
        ),
        name="head_parts",
    )(place, summaries, rider, *pieces)


def shards(summaries, head, partner):
    core = lax.axis_index("c")
    place = jnp.stack([lax.axis_index(a) for a in ("x", "zl", "y", "zh", "c")]).astype(I32)
    mates = partner.reshape(16, 1, ROWS)

    turned = summaries.T
    mine = lax.dynamic_slice_in_dim(turned, core * HALF, HALF, 1)
    theirs = core_swap(lax.dynamic_slice_in_dim(turned, (1 - core) * HALF, HALF, 1))
    other_head = core_swap(head)
    first_dims = (((0,), (0,)), ((), ()))
    z_part = lax.dot_general(
        mine, head, first_dims, preferred_element_type=F32
    ) + lax.dot_general(theirs, other_head, first_dims, preferred_element_type=F32)
    z_part, place, mates = lax.optimization_barrier((z_part.astype(BF16), place, mates))
    z = sum_exchange(z_part.reshape(8, ROWS, WIDTH), YZ)
    inv = lax.rsqrt(jnp.sum(z * z, axis=1, keepdims=True) + 1e-06)
    unit = z * inv
    emb = unit.astype(BF16)

    keys = gather_ring(emb, "x", "zl", direct=True)
    queries = gather_ring(emb, "y", "zh")
    queries = queries + [core_swap(piece) for piece in queries]
    weights, row_part, hits, col_part, queries = score_call(place, keys, queries, mates)

    cols = lax.all_to_all(col_part, CUTS, 0, 0)
    row_part = row_part + lax.ppermute(row_part, "zl", SWAP)
    rows = [row_part] + [lax.ppermute(row_part, "x", RING[s]) for s in (1, 3, 2)]
    grad_part, rider = grad_call(place, weights, hits, rows, cols, mates, queries)
    grad_emb = sum_exchange(grad_part.reshape(8, ROWS, WIDTH), XZ)
    grad_z = (inv * (grad_emb - unit * jnp.sum(unit * grad_emb, axis=1, keepdims=True))).astype(BF16)

    pieces = gather_ring(grad_z, "y", "zh")
    pieces = pieces + [core_swap(piece) for piece in pieces]
    head_part, grad_group = head_call(place, turned, rider, pieces)
    pieces = lax.all_to_all(head_part, XZ, 0, 0)
    pieces = jnp.sum(pieces.astype(F32), axis=0)
    features = head.shape[0]
    loss = jnp.sum(pieces[features:, 0]) / TOTAL
    head_sum = pieces[:features].astype(BF16)
    grad_head = spread(head_sum, XZ, 8).transpose(1, 0, 2).reshape(features, WIDTH).astype(F32)

    last_dims = (((1,), (1,)), ((), ()))
    out = lax.dot_general(head, grad_group, last_dims, preferred_element_type=F32).astype(BF16)
    return loss, out.T, grad_head


def solution(mesh):
    fine = Mesh(mesh.devices.reshape(4, 2, 4, 2, 2), ("x", "zl", "y", "zh", "c"))
    return jax.shard_map(
        shards,
        mesh=fine,
        in_specs=(P(XZ, CUTS), P(CUTS, None), P(XZ)),
        out_specs=(P(), P(XZ, CUTS), P(CUTS, None)),
        check_vma=False,
    )
```
